256 devices in a mesh: dp: 8 (over y, z_lo), expert: 32 (over x, z_hi, core).
Axes of the slice: x: 4, y: 4, z: 8 (z_hi: 4, z_lo: 2; z = z_hi * 2 + z_lo), core: 2. Of those that a mesh axis runs over, the one named last changes fastest.
Arguments:
- tokens: bfloat16 [8, 2048, 4096], P('dp', 'expert'), may hold values from -6 to 6, as said below
- out_grad: bfloat16 [8, 2048, 4096], P('dp', 'expert'), may hold values from -0.75 to 0.75
- router: bfloat16 [4096, 32], replicated, may hold values from -0.09375 to 0.09375
- choice_index: int32 [8, 32, 32], P('dp'), may hold values from 0 to 2047, as said below
- gate_weight: bfloat16 [32, 1536, 4096], P('expert', 'dp'), as said below
- up_weight: bfloat16 [32, 1536, 4096], P('expert', 'dp'), as said below
- down_weight: bfloat16 [32, 1536, 4096], P('expert', None, 'dp'), as said below
Outputs:
- mixed: bfloat16 [8, 2048, 4096], P('dp', 'expert')
- token_grad: bfloat16 [8, 2048, 4096], P('dp', 'expert')
- router_grad: float32 [4096, 32], replicated
- gate_grad: bfloat16 [32, 1536, 4096], P('expert', 'dp')
- up_grad: bfloat16 [32, 1536, 4096], P('expert', 'dp')
- down_grad: bfloat16 [32, 1536, 4096], P('expert', None, 'dp')
The draws below stay inside these ranges and needn't reach their ends.
Inputs may be any that keep to these rules, and one draw needn't show every extreme that they name: `tokens`: each entry is an FP4 (E2M1) value times a power of two shared by each aligned block of 16 entries along the last dimension, times a fixed power of two. `gate_weight`: each entry is an FP4 (E2M1) value times a power of two shared by each aligned block of 16 entries along the last dimension, times a fixed power of two set by the fan-in. `up_weight`: as for gate_weight. `down_weight`: as for gate_weight. `choice_index`: each list of 32 indices names distinct tokens of its group; at most 2 of them lie among the 64 tokens of one device, and in every list some device has exactly 2.
All inputs are finite; a program needn't handle non-finite values.
Results may differ from the reference program's by a relative error of at most 0.0064.
Values may be sent and summed in bfloat16 or wider, within the bound.
No kernel may reach another device: no remote copies, remote signals or barrier semaphores. Data moves between devices by JAX's collectives and lax.ppermute only.
A program may use at most 64 MiB of HBM per device.

```python
import math
import jax
import jax.numpy as jnp
from jax import lax

D = 4096
FF = 1536
CAP = 32
MOST = 2
TOK_DEV = 64
GTOK = 2048
GROUPS = 8
EXPERTS = 32


def block_values(key, shape, tensor_scale, top_exponent):
    code_key, exp_key, sign_key = jax.random.split(key, 3)
    magnitudes = jnp.array([0.0, 0.5, 1.0, 1.5, 2.0, 3.0, 4.0, 6.0], jnp.float32)
    code_ids = jax.random.randint(code_key, shape, 0, 8)
    sign_values = jnp.where(jax.random.randint(sign_key, shape, 0, 2) == 1, -1.0, 1.0)
    block_shape = shape[:-1] + (shape[-1] // 16,)
    exponents = jax.random.randint(exp_key, block_shape, -2, top_exponent + 1)
    block_scale = jnp.repeat(jnp.exp2(exponents.astype(jnp.float32)), 16, axis=-1)
    return magnitudes[code_ids] * sign_values * block_scale * tensor_scale


def fan_scale(fan_in):
    return 2.0 ** (-math.floor(math.log2(3.37 * math.sqrt(fan_in)) + 0.5))


def draw_tokens(key, part):
    key = jax.random.fold_in(key, 17)
    values = block_values(key, (GROUPS, GTOK, D), 0.25, 1)
    return values.astype(jnp.bfloat16)


def draw_gate_weight(key, part):
    key = jax.random.fold_in(key, 21)
    values = block_values(key, (EXPERTS, FF, D), fan_scale(D), 1)
    return values.astype(jnp.bfloat16)


def draw_up_weight(key, part):
    key = jax.random.fold_in(key, 22)
    values = block_values(key, (EXPERTS, FF, D), fan_scale(D), 1)
    return values.astype(jnp.bfloat16)


def draw_down_weight(key, part):
    key = jax.random.fold_in(key, 23)
    values = block_values(key, (EXPERTS, FF, D), fan_scale(FF), 1)
    return values.astype(jnp.bfloat16)


def draw_choice_index(key, part):
    key = jax.random.fold_in(key, 31)
    sources = GTOK // TOK_DEV
    pairs = sources * MOST
    lists = GROUPS * EXPERTS
    score_key, force_key, first_key, step_key = jax.random.split(key, 4)
    scores = jax.random.randint(score_key, (lists, pairs), 0, 2 ** 20) * pairs + jnp.arange(pairs, dtype=jnp.int32)[None, :]
    forced = jax.random.randint(force_key, (lists, 1), 0, sources)
    pair_ids = jnp.arange(pairs, dtype=jnp.int32)[None, :]
    scores = jnp.where(pair_ids // MOST == forced, pair_ids % MOST - MOST, scores)
    chosen = jnp.argsort(scores, axis=1)[:, :CAP].astype(jnp.int32)
    owner_dev = chosen // MOST
    slot_num = chosen % MOST
    first_off = jax.random.randint(first_key, (lists, sources), 0, TOK_DEV)
    step_off = jax.random.randint(step_key, (lists, sources), 1, TOK_DEV)
    second_off = (first_off + step_off) % TOK_DEV
    off_first = jnp.take_along_axis(first_off, owner_dev, axis=1)
    off_second = jnp.take_along_axis(second_off, owner_dev, axis=1)
    offsets = jnp.where(slot_num == 0, off_first, off_second)
    picked = owner_dev * TOK_DEV + offsets
    return picked.reshape(GROUPS, EXPERTS, CAP).astype(jnp.int32)


def shard_levels(own_key, shape, cuts, least, high):
    def one(axis_at, blocks):
        draws = jax.random.uniform(jax.random.fold_in(jax.random.fold_in(own_key, 6), axis_at), (blocks,), jnp.float32, least / len(cuts), high / len(cuts))
        return jnp.repeat(jnp.exp(draws), shape[axis_at] // blocks).reshape((-1,) + (1,) * (len(shape) - axis_at - 1))

    factor_of = one(*cuts[0])
    for cut in cuts[1:]:
        factor_of = factor_of * one(*cut)
    return factor_of


def gaussian(stream_key, extent, scale, limit, cuts=(), kind=jnp.bfloat16):
    drawn = jax.random.normal(stream_key, extent, jnp.float32) * scale
    if len(cuts) > 0:
        drawn = shard_levels(stream_key, extent, cuts, -0.22, 0.18) * drawn
    return jnp.clip(drawn, min=-limit, max=limit).astype(kind)


def setup_inputs(seed: int = 0) -> dict:
    seeds = jax.random.split(jax.random.key(seed), 8)
    tokens = draw_tokens(jax.random.fold_in(seeds[7], 71), 0)
    out_grad = gaussian(seeds[1], (GROUPS, GTOK, D), 0.125, 0.75, ((0, 8), (1, 32)))
    router = gaussian(seeds[2], (D, EXPERTS), D ** -0.5, 0.09375)
    choice_index = draw_choice_index(jax.random.fold_in(seeds[7], 71), 0)
    gate_weight = draw_gate_weight(jax.random.fold_in(seeds[7], 71), 0)
    up_weight = draw_up_weight(jax.random.fold_in(seeds[7], 71), 0)
    down_weight = draw_down_weight(jax.random.fold_in(seeds[7], 71), 0)
    return {"tokens": tokens, "out_grad": out_grad, "router": router, "choice_index": choice_index, "gate_weight": gate_weight, "up_weight": up_weight, "down_weight": down_weight}


def reference(tokens, out_grad, router, choice_index, gate_weight, up_weight, down_weight):
    groups = tokens.shape[0]
    highest = lax.Precision.HIGHEST
    logits = jnp.einsum('gtd,de->gte', tokens.astype(jnp.float32), router.astype(jnp.float32))
    gates = jax.nn.sigmoid(logits)
    group_ids = jnp.arange(groups, dtype=jnp.int32)[:, None]

    def expert_pass(expert):
        picked = choice_index[:, expert, :]
        rows_in = tokens[group_ids, picked].reshape(groups * CAP, D)
        grads_in = out_grad[group_ids, picked]
        gate_here = gates[:, :, expert][group_ids, picked]
        gated = (gate_here[:, :, None] * grads_in.astype(jnp.float32)).astype(jnp.bfloat16).reshape(groups * CAP, D)
        w_gate = gate_weight[expert]
        w_up = up_weight[expert]
        w_down = down_weight[expert]
        hidden_pre = jnp.dot(rows_in, w_gate.T, preferred_element_type=jnp.float32)
        up_pre = jnp.dot(rows_in, w_up.T, preferred_element_type=jnp.float32)
        activated = (jax.nn.silu(hidden_pre) * up_pre).astype(jnp.bfloat16)
        expert_out = jnp.dot(activated, w_down, preferred_element_type=jnp.float32).astype(jnp.bfloat16)
        gate_diff = jnp.sum(grads_in.astype(jnp.float32) * expert_out.reshape(groups, CAP, D).astype(jnp.float32), axis=2)
        act_diff = jnp.dot(gated, w_down.T, preferred_element_type=jnp.float32)
        sigma = jax.nn.sigmoid(hidden_pre)
        hidden_diff = (act_diff * up_pre * sigma * (1.0 + hidden_pre * (1.0 - sigma))).astype(jnp.bfloat16)
        up_diff = (act_diff * hidden_pre * sigma).astype(jnp.bfloat16)
        down_diff = jnp.dot(activated.T, gated, preferred_element_type=jnp.float32).astype(jnp.bfloat16)
        gate_diff_w = jnp.dot(hidden_diff.T, rows_in, preferred_element_type=jnp.float32).astype(jnp.bfloat16)
        up_diff_w = jnp.dot(up_diff.T, rows_in, preferred_element_type=jnp.float32).astype(jnp.bfloat16)
        rows_diff = (jnp.dot(hidden_diff, w_gate, preferred_element_type=jnp.float32)
                     + jnp.dot(up_diff, w_up, preferred_element_type=jnp.float32)).astype(jnp.bfloat16)
        return expert_out, rows_diff, gate_here, gate_diff, gate_diff_w, up_diff_w, down_diff

    outs_all, rows_all, gate_all, gdiff_all, gate_grad, up_grad, down_grad = lax.map(
        expert_pass, jnp.arange(EXPERTS, dtype=jnp.int32))
    token_ids = jnp.transpose(choice_index, (1, 0, 2))
    group_full = jnp.broadcast_to(jnp.arange(groups, dtype=jnp.int32)[None, :, None], token_ids.shape)
    expert_full = jnp.broadcast_to(jnp.arange(EXPERTS, dtype=jnp.int32)[:, None, None], token_ids.shape)
    outs_all = outs_all.reshape(EXPERTS, groups, CAP, D).astype(jnp.float32)
    rows_all = rows_all.reshape(EXPERTS, groups, CAP, D).astype(jnp.float32)
    mixed = jnp.zeros(tokens.shape, jnp.float32).at[group_full, token_ids].add(gate_all[..., None] * outs_all)
    logit_diff = jnp.zeros(gates.shape, jnp.float32).at[group_full, token_ids, expert_full].add(
        gdiff_all * gate_all * (1.0 - gate_all))
    router_grad = jnp.einsum('gtd,gte->de', tokens.astype(jnp.float32), logit_diff, precision=highest)
    token_grad = jnp.zeros(tokens.shape, jnp.float32).at[group_full, token_ids].add(rows_all)
    token_grad = token_grad + jnp.einsum('gte,de->gtd', logit_diff, router.astype(jnp.float32), precision=highest)
    return (mixed.astype(jnp.bfloat16), token_grad.astype(jnp.bfloat16), router_grad,
            gate_grad, up_grad, down_grad)
```

```python
import functools

import jax
import jax.numpy as jnp
from jax import lax
from jax.experimental import pallas as pl
from jax.experimental.pallas import tpu as pltpu
from jax.sharding import PartitionSpec as P

MOST = 2
QUARTERS = 4
F32 = jnp.float32
BF16 = jnp.bfloat16
VMEM = pl.BlockSpec(memory_space=pltpu.VMEM)
SMEM = pl.BlockSpec(memory_space=pltpu.SMEM)


def iota(shape, dim):
    return lax.broadcasted_iota(jnp.int32, shape, dim)


def nn(a, b):
    return lax.dot_general(a, b, (((1,), (0,)), ((), ())), preferred_element_type=F32)


def nt(a, b):
    return lax.dot_general(a, b, (((1,), (1,)), ((), ())), preferred_element_type=F32)


def tn(a, b):
    return lax.dot_general(a, b, (((0,), (0,)), ((), ())), preferred_element_type=F32)


def pieces(x):
    hi = x.astype(BF16)
    rest = x - hi.astype(F32)
    mid = rest.astype(BF16)
    low = (rest - mid.astype(F32)).astype(BF16)
    return hi, mid, low


def call(kernel, outs, args, limit=40, **params):
    return pl.pallas_call(
        kernel,
        out_shape=tuple(jax.ShapeDtypeStruct(s, d) for s, d in outs),
        in_specs=[SMEM if a.ndim == 1 else VMEM for a in args],
        out_specs=tuple(VMEM for _ in outs),
        compiler_params=pltpu.CompilerParams(vmem_limit_bytes=limit * 2**20),
        **params,
    )(*args)


def send_kernel(src_ref, table_ref, tok_ref, grad_ref, router_ref, x_ref, sel_ref, gsel_ref, gates_ref):
    tok_count, width = tok_ref.shape
    experts, cap = table_ref.shape
    part = width // QUARTERS
    slots = experts * MOST * QUARTERS
    gates = jax.nn.sigmoid(nn(tok_ref[...], router_ref[...]))
    gates_ref[...] = gates
    table = table_ref[...]
    owner = table // tok_count
    offset = table - owner * tok_count
    mine = (owner == src_ref[0]).astype(F32)
    before = (iota((cap, cap), 0) < iota((cap, cap), 1)).astype(BF16)
    rank = nn(mine.astype(BF16), before)
    col = iota((experts, slots), 1)
    own_col = (col // (MOST * QUARTERS)) == iota((experts, slots), 0)
    col_rank = (col // QUARTERS) % MOST
    wanted = jnp.zeros((1, slots), F32)
    for m in range(MOST):
        chosen = jnp.sum(
            jnp.where(rank == m, mine, 0.0) * (offset + 1).astype(F32), axis=1, keepdims=True
        )
        wanted += jnp.sum(
            jnp.where(own_col & (col_rank == m), chosen, 0.0), axis=0, keepdims=True
        )
    sel = (iota((tok_count, slots), 0) + 1).astype(F32) == wanted
    expand = own_col.astype(BF16)
    gate_exp = sum(nn(p, expand) for p in pieces(gates))
    gsel = jnp.where(sel, gate_exp, 0.0)
    sel_low = sel.astype(BF16)
    sel_ref[...] = sel_low
    gsel_ref[...] = gsel
    ones = jnp.ones((tok_count, 128), BF16)
    slot_gate = sum(tn(p, ones) for p in pieces(gsel))
    quarter = iota((tok_count, slots), 1) % QUARTERS
    pick = jnp.concatenate(
        [jnp.where(quarter == q, sel_low, jnp.zeros_like(sel_low)) for q in range(QUARTERS)], axis=0
    )
    for half, ref in enumerate((tok_ref, grad_ref)):
        rows = jnp.concatenate([ref[:, q * part : (q + 1) * part] for q in range(QUARTERS)], axis=0)
        got = tn(pick, rows)
        if half == 1:
            got = got * slot_gate[:, :1]
        x_ref[:, half * part : (half + 1) * part] = got.astype(BF16)


def own_rows(src_ref, table_ref, tok_count):
    experts, cap = table_ref.shape
    owner = table_ref[...] // tok_count
    row = jnp.sum(
        jnp.where(iota((experts, cap), 0) == src_ref[0], owner, 0).astype(F32), axis=0, keepdims=True
    )
    a, b = iota((cap, cap), 0), iota((cap, cap), 1)
    col = jnp.sum(jnp.where(a == b, row, 0.0), axis=1, keepdims=True)
    same = row == col
    rank_col = jnp.sum(jnp.where(same & (b < a), 1.0, 0.0), axis=1, keepdims=True)
    rank_row = jnp.sum(jnp.where(same & (a < b), 1.0, 0.0), axis=0, keepdims=True)
    step = MOST * QUARTERS
    return (
        (row * step + rank_row * QUARTERS).astype(jnp.int32),
        (col * step + rank_col * QUARTERS).astype(jnp.int32),
    )


def pack_kernel(tok_count, src_ref, table_ref, x_ref, a_ref):
    cap = table_ref.shape[1]
    slots, twice = x_ref.shape
    part = twice // 2
    n_dp = a_ref.shape[0]
    _, col = own_rows(src_ref, table_ref, tok_count)
    ids = jnp.concatenate([col + q for q in range(QUARTERS)], axis=0)
    pick = (iota((QUARTERS * cap, slots), 1) == ids).astype(BF16)
    y = nn(pick, x_ref[...]).astype(BF16)
    width = part * QUARTERS
    cols = width // n_dp
    for d in range(n_dp):
        for q in range(QUARTERS):
            a_ref[d, :, q * part : (q + 1) * part] = y[q * cap : (q + 1) * cap, :part]
        q, start = divmod(d * cols, part)
        a_ref[d, :, width : width + cols] = y[q * cap : (q + 1) * cap, part + start : part + start + cols]


def hidden_kernel(src_ref, a_ref, gate_ref, up_ref, down_ref, router_ref, b_ref, h_ref, u_ref, rest_ref):
    units, width = gate_ref.shape
    rows_n = a_ref.shape[0]
    n_dp = b_ref.shape[0]
    rows = a_ref[:, :width]
    h = nt(gate_ref[...], rows)
    u = nt(up_ref[...], rows)
    h_ref[...] = h
    u_ref[...] = u
    act = (h * jax.nn.sigmoid(h) * u).astype(BF16)
    gated = a_ref[:, width:]
    logits = nn(rows, router_ref[...])
    own = jnp.where(iota(logits.shape, 1) == src_ref[0], logits, 0.0)
    gate = jax.nn.sigmoid(jnp.sum(own, axis=1, keepdims=True))
    rest_ref[...] = jnp.broadcast_to(1.0 - gate, rest_ref.shape)
    for d in range(n_dp):
        b_ref[d, :, :rows_n] = act
        b_ref[d, :, rows_n:] = nt(down_ref[d * units : (d + 1) * units, :], gated).astype(BF16)


def diff_kernel(b_ref, h_ref, u_ref, a_ref, gate_ref, up_ref, down_ref, rest_ref, c_ref, dh_ref, du_ref):
    n_dp, units, twice = b_ref.shape
    rows_n = twice // 2
    width = gate_ref.shape[1]
    cap = rows_n // n_dp
    cols = down_ref.shape[1]
    dact = b_ref[0, :, rows_n:].astype(F32)
    for d in range(1, n_dp):
        dact = dact + b_ref[d, :, rows_n:].astype(F32)
    h, u = h_ref[...], u_ref[...]
    sig = jax.nn.sigmoid(h)
    dh = (dact * u * sig * (1.0 + h * (1.0 - sig))).astype(BF16)
    du = (dact * h * sig).astype(BF16)
    dh_ref[...] = dh
    du_ref[...] = du
    out = tn(b_ref[0, :, :rows_n], down_ref[:units, :])
    for d in range(1, n_dp):
        out = out + tn(b_ref[d, :, :rows_n], down_ref[d * units : (d + 1) * units, :])
    out = out.astype(BF16)
    c_ref[:, width : width + cols] = out
    dgate = jnp.sum(a_ref[:, width:].astype(F32) * out.astype(F32), axis=1, keepdims=True)
    dlogit = dgate * rest_ref[:, :1]
    lane = iota((cap, 128), 1)
    packed = jnp.zeros((cap, 128), F32)
    for p, piece in enumerate(pieces(dlogit)):
        piece = piece.astype(F32)
        for g in range(n_dp):
            packed = jnp.where(lane == p * n_dp + g, piece[g * cap : (g + 1) * cap], packed)
    c_ref[:, width + cols :] = jnp.concatenate([packed] * n_dp, axis=0).astype(BF16)
    dht, dut = dh.T, du.T
    step = 512
    for j in range(0, width, step):
        c_ref[:, j : j + step] = (
            nn(dht, gate_ref[:, j : j + step]) + nn(dut, up_ref[:, j : j + step])
        ).astype(BF16)


def weight_kernel(dh_ref, du_ref, b_ref, a_ref, gg_ref, ug_ref, dg_ref):
    units, width = gg_ref.shape
    n_dp = b_ref.shape[0]
    rows_n = a_ref.shape[0]
    step = 512
    dh, du = dh_ref[...], du_ref[...]
    for j in range(0, width, step):
        gg_ref[:, j : j + step] = nn(dh, a_ref[:, j : j + step]).astype(BF16)
        ug_ref[:, j : j + step] = nn(du, a_ref[:, j : j + step]).astype(BF16)
    gated = a_ref[:, width:]
    for d in range(n_dp):
        dg_ref[d * units : (d + 1) * units, :] = nn(b_ref[d, :, :rows_n], gated).astype(BF16)


def back_kernel(tok_count, src_ref, table_ref, c_ref, a_ref, z_ref):
    n_dp, cap, _ = c_ref.shape
    slots = z_ref.shape[0]
    part = 1024
    width = part * QUARTERS
    cols = width // n_dp
    row, _ = own_rows(src_ref, table_ref, tok_count)
    ids = jnp.concatenate([row + q for q in range(QUARTERS)], axis=1)
    place = (iota((slots, QUARTERS * cap), 0) == ids).astype(BF16)
    per = part // cols
    outs = jnp.concatenate(
        [
            jnp.concatenate([c_ref[q * per + i, :, width : width + cols] for i in range(per)], axis=1)
            for q in range(QUARTERS)
        ],
        axis=0,
    )
    z_ref[:, :part] = nn(place, outs).astype(BF16)
    diffs = []
    for q in range(QUARTERS):
        total = c_ref[0, :, q * part : (q + 1) * part].astype(F32)
        for d in range(1, n_dp):
            total = total + c_ref[d, :, q * part : (q + 1) * part].astype(F32)
        diffs.append(total.astype(BF16))
    z_ref[:, part : 2 * part] = nn(place, jnp.concatenate(diffs, axis=0)).astype(BF16)
    packed = c_ref[0, :, width + cols :].astype(F32)
    for d in range(1, n_dp):
        packed = packed + c_ref[d, :, width + cols :].astype(F32)
    rows_n = n_dp * cap
    lane = iota((128, rows_n), 0)
    spread = ((lane % n_dp == iota((128, rows_n), 1) // cap) & (lane < 3 * n_dp)).astype(BF16)
    dlogit = sum(nn(p, spread) for p in pieces(packed))
    dlogit = jnp.sum(
        jnp.where(iota((cap, rows_n), 0) == iota((cap, rows_n), 1) % cap, dlogit, 0.0),
        axis=0,
        keepdims=True,
    )
    terms = jnp.concatenate(
        [p.astype(F32) for p in pieces(dlogit)] + [jnp.zeros((5, rows_n), F32)], axis=0
    ).astype(BF16)
    chunk = width // 8
    column = jnp.concatenate(
        [
            jnp.sum(nn(terms, a_ref[:, i * chunk : (i + 1) * chunk]), axis=0, keepdims=True)
            for i in range(8)
        ],
        axis=0,
    )
    z_ref[:, 2 * part :] = jnp.concatenate([column] * (slots // 8), axis=0).astype(BF16)


def take_kernel(d_ref, sel_ref, gsel_ref, gates_ref, grad_ref, router_ref, mixed_ref, tgrad_ref):
    tok_count, width = grad_ref.shape
    slots = d_ref.shape[0]
    experts = gates_ref.shape[1]
    part = width // QUARTERS
    sel, gsel = sel_ref[...], gsel_ref[...]
    quarter = iota((tok_count, slots), 1) % QUARTERS
    outs = d_ref[:, :part]
    weights = pieces(gsel)
    zero = jnp.zeros_like(sel)
    hits = jnp.zeros((tok_count, slots), F32)
    for q in range(QUARTERS):
        here = quarter == q
        hits += jnp.where(here, nt(grad_ref[:, q * part : (q + 1) * part], outs), 0.0)
        mixed_ref[:, q * part : (q + 1) * part] = sum(
            nn(jnp.where(here, w, zero), outs) for w in weights
        ).astype(BF16)
    hits = jnp.where(sel != 0, hits, 0.0)
    collect = (iota((slots, experts), 0) // (MOST * QUARTERS) == iota((slots, experts), 1)).astype(BF16)
    gates = gates_ref[...]
    dlogit = sum(nn(p, collect) for p in pieces(hits)) * gates * (1.0 - gates)
    terms = pieces(dlogit)
    for q in range(QUARTERS):
        span = slice(q * part, (q + 1) * part)
        total = nn(jnp.where(quarter == q, sel, zero), d_ref[:, part : 2 * part])
        for w in terms:
            total = total + nt(w, router_ref[span, :])
        tgrad_ref[:, span] = total.astype(BF16)


def local(tokens, out_grad, router, choice_index, gate_weight, up_weight, down_weight):
    tok, grad, table = tokens[0], out_grad[0], choice_index[0]
    gate, up, down = gate_weight[0], up_weight[0], down_weight[0]
    tok_count, width = tok.shape
    experts, cap = table.shape
    units, cols = gate.shape[0], down.shape[1]
    n_dp = lax.axis_size("dp")
    rows_n = n_dp * cap
    slots = experts * MOST * QUARTERS
    src = lax.axis_index("expert").astype(jnp.int32).reshape(1)

    def swap(x, axis):
        return lax.all_to_all(x, axis, split_axis=0, concat_axis=0, tiled=True)

    x, sel, gsel, gates = call(
        send_kernel,
        [
            ((slots, width // 2), BF16),
            ((tok_count, slots), BF16),
            ((tok_count, slots), F32),
            ((tok_count, experts), F32),
        ],
        (src, table, tok, grad, router),
    )
    x = swap(x.reshape(experts, MOST * QUARTERS, width // 2), "expert").reshape(x.shape)
    (a,) = call(
        functools.partial(pack_kernel, tok_count),
        [((n_dp, cap, width + cols), BF16)],
        (src, table, x),
    )
    a = swap(a, "dp").reshape(rows_n, width + cols)
    b, h, u, rest = call(
        hidden_kernel,
        [
            ((n_dp, units, 2 * rows_n), BF16),
            ((units, rows_n), F32),
            ((units, rows_n), F32),
            ((rows_n, 128), F32),
        ],
        (src, a, gate, up, down, router),
    )
    b = swap(b, "dp")
    c, dh, du = call(
        diff_kernel,
        [
            ((rows_n, width + cols + 128), BF16),
            ((units, rows_n), BF16),
            ((units, rows_n), BF16),
        ],
        (b, h, u, a, gate, up, down, rest),
    )
    c = swap(c.reshape(n_dp, cap, width + cols + 128), "dp")
    gate_grad, up_grad, down_grad = call(
        weight_kernel,
        [((units, width), BF16), ((units, width), BF16), ((n_dp * units, cols), BF16)],
        (dh, du, b, a),
    )
    (z,) = call(
        functools.partial(back_kernel, tok_count),
        [((slots, width // 2 + width // 8), BF16)],
        (src, table, c, a),
    )
    z = swap(z.reshape(experts, MOST * QUARTERS, -1), "expert")
    router_grad = z[:, :, width // 2 :].reshape(experts, width).T.astype(F32)
    mixed, token_grad = call(
        take_kernel,
        [((tok_count, width), BF16), ((tok_count, width), BF16)],
        (z.reshape(slots, -1), sel, gsel, gates, grad, router),
    )
    return (
        mixed[None],
        token_grad[None],
        router_grad,
        gate_grad[None],
        up_grad[None],
        down_grad[None],
    )


def solution(mesh):
    in_specs = (
        P("dp", "expert", None),
        P("dp", "expert", None),
        P(),
        P("dp", None, None),
        P("expert", "dp", None),
        P("expert", "dp", None),
        P("expert", None, "dp"),
    )
    out_specs = (
        P("dp", "expert", None),
        P("dp", "expert", None),
        P(),
        P("expert", "dp", None),
        P("expert", "dp", None),
        P("expert", None, "dp"),
    )
    return jax.shard_map(local, mesh=mesh, in_specs=in_specs, out_specs=out_specs, check_vma=False)
```

```python
import jax
import jax.numpy as jnp
from jax import lax
from jax.experimental import pallas as pl
from jax.experimental.pallas import tpu as pltpu
from jax.sharding import PartitionSpec as P

MOST = 2
LANES = 128
EMPTY = 1024.0
F32 = jnp.float32
BF16 = jnp.bfloat16
VMEM = pl.BlockSpec(memory_space=pltpu.VMEM)
SMEM = pl.BlockSpec(memory_space=pltpu.SMEM)
FAR = pl.BlockSpec(memory_space=pltpu.HBM)


def iota(shape, dim):
    return lax.broadcasted_iota(jnp.int32, shape, dim)


def nn(a, b):
    return lax.dot_general(a, b, (((1,), (0,)), ((), ())), preferred_element_type=F32)


def nt(a, b):
    return lax.dot_general(a, b, (((1,), (1,)), ((), ())), preferred_element_type=F32)


def tn(a, b):
    return lax.dot_general(a, b, (((0,), (0,)), ((), ())), preferred_element_type=F32)


def pieces(x):
    hi = x.astype(BF16)
    rest = x - hi.astype(F32)
    mid = rest.astype(BF16)
    low = (rest - mid.astype(F32)).astype(BF16)
    return hi, mid, low


def call(kernel, outs, args, far_in=(), far_out=(), scratch=()):
    args = [
        pltpu.with_memory_space_constraint(a, pltpu.HBM) if i in far_in else a for i, a in enumerate(args)
    ]
    return pl.pallas_call(
        kernel,
        out_shape=tuple(
            pltpu.HBM(s, d) if i in far_out else jax.ShapeDtypeStruct(s, d)
            for i, (s, d) in enumerate(outs)
        ),
        in_specs=[SMEM if a.ndim == 1 else FAR if i in far_in else VMEM for i, a in enumerate(args)],
        out_specs=tuple(FAR if i in far_out else VMEM for i in range(len(outs))),
        scratch_shapes=scratch,
        compiler_params=pltpu.CompilerParams(vmem_limit_bytes=40 * 2**20),
    )(*args)


def send_kernel(src_ref, *refs):
    far, x_ref, outs_far, near, near_out, sem = refs[:4], refs[4], refs[5:8], refs[8:12], refs[12:15], refs[15]
    sel_ref, gsel_ref, gates_ref = near_out
    back = [
        pltpu.make_async_copy(a, b, sem.at[len(far) + i])
        for i, (a, b) in enumerate(zip(near_out, outs_far))
    ]
    copies = [pltpu.make_async_copy(a, b, sem.at[i]) for i, (a, b) in enumerate(zip(far, near))]
    for copy in copies:
        copy.start()
    table_ref, tok_ref, grad_ref, router_ref = near
    tok_count, width = tok_ref.shape
    experts, cap = table_ref.shape
    n_dp, slots, _ = x_ref.shape
    chunks = slots // (experts * MOST)
    cols = width // n_dp
    copies[0].wait()
    table = table_ref[...]
    owner = table // tok_count
    offset = table - owner * tok_count
    mine = (owner == src_ref[0]).astype(F32)
    before = (iota((cap, cap), 0) < iota((cap, cap), 1)).astype(BF16)
    rank = nn(mine.astype(BF16), before)
    col = iota((experts, slots), 1)
    own_col = (col // (MOST * chunks)) == iota((experts, slots), 0)
    col_rank = (col // chunks) % MOST
    wanted = jnp.zeros((1, slots), F32)
    for m in range(MOST):
        chosen = jnp.sum(
            jnp.where(rank == m, mine, 0.0) * (offset + 1).astype(F32), axis=1, keepdims=True
        )
        wanted += jnp.sum(
            jnp.where(own_col & (col_rank == m), chosen, 0.0), axis=0, keepdims=True
        )
    sel = (iota((tok_count, slots), 0) + 1).astype(F32) == wanted
    copies[3].wait()
    copies[1].wait()
    gates = jax.nn.sigmoid(nt(tok_ref[...], router_ref[...]))
    gates_ref[...] = gates
    expand = own_col.astype(BF16)
    gate_exp = sum(nn(p, expand) for p in pieces(gates))
    gsel = jnp.where(sel, gate_exp, 0.0)
    sel_low = sel.astype(BF16)
    sel_ref[...] = sel_low
    gsel_ref[...] = gsel
    for copy in back:
        copy.start()
    ones = jnp.ones((tok_count, LANES), BF16)
    slot_gate = sum(tn(p, ones) for p in pieces(gsel))
    slot_empty = (1.0 - tn(sel_low, ones)) * EMPTY
    chunk = iota((tok_count, slots), 1) % chunks
    pick = jnp.concatenate(
        [jnp.where(chunk == c, sel_low, jnp.zeros_like(sel_low)) for c in range(chunks)], axis=0
    )
    copies[2].wait()
    for d in range(n_dp):
        parts = []
        for c in range(chunks):
            span = slice(d * cols + c * LANES, d * cols + (c + 1) * LANES)
            parts.append(jnp.concatenate([tok_ref[:, span], grad_ref[:, span]], axis=1))
        got = tn(pick, jnp.concatenate(parts, axis=0))
        x_ref[d, :, :LANES] = (got[:, :LANES] + slot_empty).astype(BF16)
        x_ref[d, :, LANES:] = (got[:, LANES:] * slot_gate).astype(BF16)
    for copy in back:
        copy.wait()


def pack_kernel(x_ref, down_ref, p_ref, gated_ref, pick_ref):
    n_dp, rows_all, cols = p_ref.shape
    rows_n = gated_ref.shape[0]
    half = rows_all - rows_n
    cap = rows_n // n_dp
    chunks = cols // LANES
    slots = x_ref.shape[0] // n_dp
    lane = iota((slots, LANES), 1)
    row = iota((slots, LANES), 0)
    held = [x_ref[g * slots : (g + 1) * slots, :LANES] < EMPTY / 2 for g in range(n_dp)]
    a, b = iota((slots, slots), 0), iota((slots, slots), 1)
    before = ((b // chunks < a // chunks) & (b % chunks == 0)).astype(BF16)
    place = nn(before, jnp.concatenate([h.astype(BF16) for h in held], axis=1))
    mine = lane // cap == row % chunks
    want = (lane % cap).astype(F32)
    for g in range(n_dp):
        at = jnp.where(mine, place[:, g * LANES : (g + 1) * LANES], -1.0)
        pick = jnp.where(at == want, held[g].astype(F32), 0.0).astype(BF16)
        pick_ref[g * slots : (g + 1) * slots, :] = pick
        y = tn(pick, x_ref[g * slots : (g + 1) * slots, :]).astype(BF16)
        own = slice(g * cap, (g + 1) * cap)
        for c in range(chunks):
            span = slice(c * LANES, (c + 1) * LANES)
            gated_ref[own, span] = y[c * cap : (c + 1) * cap, LANES:]
            for d in range(n_dp):
                p_ref[d, own, span] = y[c * cap : (c + 1) * cap, :LANES]
    gated = gated_ref[...]
    for d in range(n_dp):
        term = nt(down_ref[2 * d * half : 2 * (d + 1) * half, :], gated).astype(BF16)
        p_ref[d, rows_n:, :rows_n] = term[:half]
        p_ref[d, rows_n:, rows_n:] = term[half:]


def hidden_kernel(src_ref, a_ref, gate_ref, up_ref, router_ref, c_ref, dh_ref, du_ref):
    units, width = gate_ref.shape
    experts = router_ref.shape[0]
    n_dp, rows_all, cols = a_ref.shape
    half = units // 2
    rows_n = rows_all - half
    total = jnp.zeros((2 * units + experts, rows_n), F32)
    dact = jnp.zeros((units, rows_n), F32)
    group = 2
    for d in range(0, n_dp, group):
        span = slice(d * cols, (d + group) * cols)
        left = jnp.concatenate([gate_ref[:, span], up_ref[:, span], router_ref[:, span]], axis=0)
        rows = jnp.concatenate([a_ref[d + i, :rows_n, :] for i in range(group)], axis=1)
        total += nt(left, rows)
    for d in range(n_dp):
        term = a_ref[d, rows_n:, :].astype(F32)
        dact += jnp.concatenate([term[:, :rows_n], term[:, rows_n:]], axis=0)
    h, u, logits = total[:units], total[units : 2 * units], total[2 * units :]
    own = jnp.where(iota(logits.shape, 0) == src_ref[0], logits, 0.0)
    gate = jax.nn.sigmoid(jnp.sum(own, axis=0, keepdims=True))
    sig = jax.nn.sigmoid(h)
    act = (h * sig * u).astype(BF16)
    dh = (dact * u * sig * (1.0 + h * (1.0 - sig))).astype(BF16)
    du = (dact * h * sig).astype(BF16)
    dh_ref[...] = dh
    du_ref[...] = du
    dlogit = jnp.sum(act.astype(F32) * dact, axis=0, keepdims=True) * (1.0 - gate)
    lines = [p.astype(F32) for p in pieces(dlogit)]
    extra = c_ref.shape[1] - rows_all
    lines.append(jnp.zeros((extra - len(lines), rows_n), F32))
    lines = jnp.concatenate(lines, axis=0)
    lines = jnp.concatenate([lines, jnp.zeros((extra, cols - rows_n), F32)], axis=1).astype(BF16)
    dht, dut = dh.T, du.T
    for d in range(n_dp):
        span = slice(d * cols, (d + 1) * cols)
        c_ref[d, :rows_n, :] = (nn(dht, gate_ref[:, span]) + nn(dut, up_ref[:, span])).astype(BF16)
        c_ref[d, rows_n:rows_all, :rows_n] = act[:half]
        c_ref[d, rows_n:rows_all, rows_n:] = act[half:]
        c_ref[d, rows_all:, :] = lines


def back_kernel(c_ref, a_ref, down_ref, pick_ref, z_out, r_ref, act_out, z_ref, act_ref, sem):
    n_dp, rows_all, cols = a_ref.shape
    half = act_ref.shape[0] // (2 * n_dp)
    rows_n = rows_all - half
    cap = rows_n // n_dp
    chunks = cols // LANES
    slots = z_ref.shape[0] // n_dp
    diff = jnp.zeros((rows_n, cols), F32)
    packed = jnp.zeros((c_ref.shape[1] - rows_all, cols), F32)
    for d in range(n_dp):
        act_ref[2 * d * half : (2 * d + 1) * half, :] = c_ref[d, rows_n:rows_all, :rows_n]
        act_ref[(2 * d + 1) * half : 2 * (d + 1) * half, :] = c_ref[d, rows_n:rows_all, rows_n:]
        diff += c_ref[d, :rows_n, :].astype(F32)
        packed += c_ref[d, rows_all:, :].astype(F32)
    copies = [pltpu.make_async_copy(act_ref, act_out, sem.at[n_dp])]
    copies[0].start()
    diff = diff.astype(BF16)
    out = tn(act_ref[...], down_ref[...]).astype(BF16)
    for g in range(n_dp):
        own = slice(g * cap, (g + 1) * cap)
        y = jnp.concatenate(
            [
                jnp.concatenate([x[own, c * LANES : (c + 1) * LANES] for x in (out, diff)], axis=1)
                for c in range(chunks)
            ],
            axis=0,
        )
        at = slice(g * slots, (g + 1) * slots)
        z_ref[at, :] = nn(pick_ref[at, :], y).astype(BF16)
        copies.append(pltpu.make_async_copy(z_ref.at[at], z_out.at[at], sem.at[g]))
        copies[-1].start()
    dlogit = packed[:1, :rows_n] + packed[1:2, :rows_n] + packed[2:3, :rows_n]
    terms = [p.astype(F32) for p in pieces(dlogit)]
    terms = jnp.concatenate(terms + [jnp.zeros((8 - len(terms), rows_n), F32)], axis=0).astype(BF16)
    part = r_ref.shape[1]
    lines = []
    for d in range(n_dp):
        line = jnp.sum(nn(terms, a_ref[d, :rows_n, :]), axis=0, keepdims=True)
        lines += [line[:, i : i + part] for i in range(0, cols, part)]
    r_ref[...] = jnp.concatenate(lines, axis=0).astype(BF16)
    for copy in copies:
        copy.wait()


def weight_kernel(dh_ref, du_ref, act_ref, gated_ref, a_ref, gg_ref, ug_ref, dg_ref):
    n_dp, _, cols = a_ref.shape
    rows_n = gated_ref.shape[0]
    dh, du, gated = dh_ref[...], du_ref[...], gated_ref[...]
    for d in range(n_dp):
        span = slice(d * cols, (d + 1) * cols)
        rows = a_ref[d, :rows_n, :]
        gg_ref[:, span] = nn(dh, rows).astype(BF16)
        ug_ref[:, span] = nn(du, rows).astype(BF16)
    step = 256
    for j in range(0, dg_ref.shape[0], step):
        dg_ref[j : j + step, :] = nn(act_ref[j : j + step, :], gated).astype(BF16)


def take_kernel(src_ref, r_ref, *refs):
    far, outs_far, near, near_out, sem = refs[:6], refs[6:9], refs[9:15], refs[15:18], refs[18]
    d_ref, sel_ref, gsel_ref, gates_ref, grad_ref, router_ref = near
    mixed_ref, tgrad_ref, rgrad_ref = near_out
    copies = [pltpu.make_async_copy(a, b, sem.at[i]) for i, (a, b) in enumerate(zip(far, near))]
    for i in (1, 2, 0, 4, 3, 5):
        copies[i].start()
    tok_count, width = grad_ref.shape
    experts = gates_ref.shape[1]
    slots = sel_ref.shape[1]
    n_dp = d_ref.shape[0] // slots
    chunks = slots // (experts * MOST)
    cols = width // n_dp
    back = [
        pltpu.make_async_copy(a, b, sem.at[len(far) + i])
        for i, (a, b) in enumerate(zip(near_out, outs_far))
    ]
    n_rows, part = r_ref.shape
    lines = n_rows // experts
    me = src_ref[0]
    me_x, me_z, me_c = me // 8, (me // 2) % 4, me % 2
    row, col = iota((n_rows, n_rows), 0), iota((n_rows, n_rows), 1)
    block = col // lines
    source = ((me_x + 4 - (block // 2) % 4) % 4) * 8 + ((me_z + 4 - block // 8) % 4) * 2 + (me_c + block) % 2
    sort = ((row % experts == source) & (row // experts == col % lines)).astype(BF16)
    rgrad = nn(sort, r_ref[...])
    for i in range(lines):
        rgrad_ref[:, i * part : (i + 1) * part] = rgrad[i * experts : (i + 1) * experts]
    back[2].start()
    chunk = iota((tok_count, slots), 1) % chunks

    def by_chunk(x):
        return jnp.concatenate(
            [jnp.where(chunk == c, x, jnp.zeros_like(x)) for c in range(chunks)], axis=0
        )

    def span(d, c):
        return slice(d * cols + c * LANES, d * cols + (c + 1) * LANES)

    copies[1].wait()
    copies[2].wait()
    pick = by_chunk(sel_ref[...])
    weights = [by_chunk(w) for w in pieces(gsel_ref[...])]
    copies[0].wait()
    outs = jnp.concatenate([d_ref[d * slots : (d + 1) * slots, :LANES] for d in range(n_dp)], axis=1)
    mixed = sum(nn(w, outs) for w in weights).astype(BF16)
    for d in range(n_dp):
        for c in range(chunks):
            mixed_ref[:, span(d, c)] = mixed[
                c * tok_count : (c + 1) * tok_count, d * LANES : (d + 1) * LANES
            ]
    back[0].start()
    copies[4].wait()
    grads = jnp.concatenate(
        [
            jnp.concatenate([grad_ref[:, span(d, c)] for d in range(n_dp)], axis=1)
            for c in range(chunks)
        ],
        axis=0,
    )
    hits = jnp.where(pick != 0, nt(grads, outs), 0.0)
    hits = sum(hits[c * tok_count : (c + 1) * tok_count] for c in range(chunks))
    collect = (iota((slots, experts), 0) // (MOST * chunks) == iota((slots, experts), 1)).astype(BF16)
    copies[3].wait()
    copies[5].wait()
    gates = gates_ref[...]
    dlogit = sum(nn(p, collect) for p in pieces(hits)) * gates * (1.0 - gates)
    terms = jnp.concatenate(pieces(dlogit), axis=1)
    diffs = jnp.concatenate([d_ref[d * slots : (d + 1) * slots, LANES:] for d in range(n_dp)], axis=1)
    diffs = nn(pick, diffs)
    for d in range(n_dp):
        router = router_ref[:, d * cols : (d + 1) * cols]
        from_router = nn(terms, jnp.concatenate([router] * 3, axis=0))
        for c in range(chunks):
            own = slice(c * tok_count, (c + 1) * tok_count)
            lanes = slice(d * LANES, (d + 1) * LANES)
            tgrad_ref[:, span(d, c)] = (
                diffs[own, lanes] + from_router[:, c * LANES : (c + 1) * LANES]
            ).astype(BF16)
    back[1].start()
    for copy in back:
        copy.wait()


def spread(r):
    def shifted(x, k, to):
        return lax.ppermute(x, "expert", [(e, to(e, k)) for e in range(32)])

    def core(e, k):
        return e // 2 * 2 + (e + k) % 2

    def along_x(e, k):
        return (e + 8 * k) % 32

    def along_z(e, k):
        return e // 8 * 8 + (e + 2 * k) % 8

    for to, n in ((core, 2), (along_x, 4), (along_z, 4)):
        r = jnp.concatenate([r] + [shifted(r, k, to) for k in range(1, n)], axis=0)
    return r


def local(tokens, out_grad, router, choice_index, gate_weight, up_weight, down_weight):
    tok, grad, table = tokens[0], out_grad[0], choice_index[0]
    gate, up, down = gate_weight[0], up_weight[0], down_weight[0]
    router = router.T
    tok_count, width = tok.shape
    experts, cap = table.shape
    units, cols = gate.shape[0], down.shape[1]
    n_dp = lax.axis_size("dp")
    rows_n = n_dp * cap
    chunks = cols // LANES
    per = MOST * chunks
    slots = experts * per
    rows_all = rows_n + units // 2
    src = lax.axis_index("expert").astype(jnp.int32).reshape(1)

    def swap(x, axis):
        return lax.all_to_all(x, axis, split_axis=0, concat_axis=0, tiled=True)

    kept = [((tok_count, slots), BF16), ((tok_count, slots), F32), ((tok_count, experts), F32)]
    x, sel, gsel, gates = call(
        send_kernel,
        [((n_dp, slots, 2 * LANES), BF16)] + kept,
        (src, table, tok, grad, router),
        far_in=(1, 2, 3, 4),
        far_out=(1, 2, 3),
        scratch=[pltpu.VMEM(a.shape, a.dtype) for a in (table, tok, grad, router)]
        + [pltpu.VMEM(s, d) for s, d in kept]
        + [pltpu.SemaphoreType.DMA((4 + len(kept),))],
    )
    x = swap(x.reshape(n_dp * experts, per, 2 * LANES), ("dp", "expert"))
    a, gated, pick = call(
        pack_kernel,
        [
            ((n_dp, rows_all, cols), BF16),
            ((rows_n, cols), BF16),
            ((n_dp * slots, LANES), BF16),
        ],
        (x.reshape(n_dp * slots, 2 * LANES), down),
    )
    a = swap(a, "dp")
    c, dh, du = call(
        hidden_kernel,
        [
            ((n_dp, rows_all + 16, cols), BF16),
            ((units, rows_n), BF16),
            ((units, rows_n), BF16),
        ],
        (src, a, gate, up, router),
    )
    c = swap(c, "dp")
    z, r, act = call(
        back_kernel,
        [
            ((n_dp * slots, 2 * LANES), BF16),
            ((16, width // 16), BF16),
            ((n_dp * units, rows_n), BF16),
        ],
        (c, a, down, pick),
        far_out=(0, 2),
        scratch=[
            pltpu.VMEM((n_dp * slots, 2 * LANES), BF16),
            pltpu.VMEM((n_dp * units, rows_n), BF16),
            pltpu.SemaphoreType.DMA((n_dp + 1,)),
        ],
    )
    z = swap(z.reshape(n_dp * experts, per, 2 * LANES), ("dp", "expert"))
    r = spread(r)
    gate_grad, up_grad, down_grad = call(
        weight_kernel,
        [((units, width), BF16), ((units, width), BF16), ((n_dp * units, cols), BF16)],
        (dh, du, act, gated, a),
    )
    taken = (z.reshape(n_dp * slots, 2 * LANES), sel, gsel, gates, grad, router)
    results = [((tok_count, width), BF16), ((tok_count, width), BF16), ((experts, width), F32)]
    mixed, token_grad, router_grad = call(
        take_kernel,
        results,
        (src, r) + taken,
        far_in=range(2, 8),
        far_out=range(3),
        scratch=[pltpu.VMEM(a.shape, a.dtype) for a in taken]
        + [pltpu.VMEM(s, d) for s, d in results]
        + [pltpu.SemaphoreType.DMA((len(taken) + len(results),))],
    )
    return (
        mixed[None],
        token_grad[None],
        router_grad.T,
        gate_grad[None],
        up_grad[None],
        down_grad[None],
    )


def solution(mesh):
    in_specs = (
        P("dp", "expert", None),
        P("dp", "expert", None),
        P(),
        P("dp", None, None),
        P("expert", "dp", None),
        P("expert", "dp", None),
        P("expert", None, "dp"),
    )
    out_specs = (
        P("dp", "expert", None),
        P("dp", "expert", None),
        P(),
        P("expert", "dp", None),
        P("expert", "dp", None),
        P("expert", None, "dp"),
    )
    return jax.shard_map(local, mesh=mesh, in_specs=in_specs, out_specs=out_specs, check_vma=False)
```

```python
import jax
import jax.numpy as jnp
from jax import lax
from jax.experimental import pallas as pl
from jax.experimental.pallas import tpu as pltpu
from jax.sharding import PartitionSpec as P

MOST = 2
LANES = 128
EMPTY = 1024.0
F32 = jnp.float32
BF16 = jnp.bfloat16
VMEM = pl.BlockSpec(memory_space=pltpu.VMEM)
SMEM = pl.BlockSpec(memory_space=pltpu.SMEM)
FAR = pl.BlockSpec(memory_space=pltpu.HBM)


def iota(shape, dim):
    return lax.broadcasted_iota(jnp.int32, shape, dim)


def nn(a, b):
    return lax.dot_general(a, b, (((1,), (0,)), ((), ())), preferred_element_type=F32)


def nt(a, b):
    return lax.dot_general(a, b, (((1,), (1,)), ((), ())), preferred_element_type=F32)


def tn(a, b):
    return lax.dot_general(a, b, (((0,), (0,)), ((), ())), preferred_element_type=F32)


def pieces(x):
    hi = x.astype(BF16)
    rest = x - hi.astype(F32)
    mid = rest.astype(BF16)
    low = (rest - mid.astype(F32)).astype(BF16)
    return hi, mid, low


def call(kernel, outs, args, far_in=(), far_out=(), scratch=()):
    args = [
        pltpu.with_memory_space_constraint(a, pltpu.HBM) if i in far_in else a for i, a in enumerate(args)
    ]
    return pl.pallas_call(
        kernel,
        out_shape=tuple(
            pltpu.HBM(s, d) if i in far_out else jax.ShapeDtypeStruct(s, d)
            for i, (s, d) in enumerate(outs)
        ),
        in_specs=[SMEM if a.ndim == 1 else FAR if i in far_in else VMEM for i, a in enumerate(args)],
        out_specs=tuple(FAR if i in far_out else VMEM for i in range(len(outs))),
        scratch_shapes=scratch,
        compiler_params=pltpu.CompilerParams(vmem_limit_bytes=40 * 2**20),
    )(*args)


def chunked(src, dst, n, sem, at):
    rows = src.shape[0] // n
    parts = [pl.ds(i * rows, rows) for i in range(n)]
    return [pltpu.make_async_copy(src.at[p], dst.at[p], sem.at[at + i]) for i, p in enumerate(parts)]


def start(copies):
    for copy in copies:
        copy.start()


def wait(copies):
    for copy in copies:
        copy.wait()


def send_kernel(src_ref, *refs):
    far, x_ref, outs_far, near, near_out, sem = refs[:4], refs[4], refs[5:8], refs[8:12], refs[12:15], refs[15]
    sel_ref, gsel_ref, gates_ref = near_out
    copies, at = [], 0
    for src, dst, n in zip(far, near, (1, 4, 4, 2)):
        copies.append(chunked(src, dst, n, sem, at))
        at += n
    back = [pltpu.make_async_copy(a, b, sem.at[at + i]) for i, (a, b) in enumerate(zip(near_out, outs_far))]
    for i in (0, 3, 1, 2):
        start(copies[i])
    table_ref, tok_ref, grad_ref, router_ref = near
    tok_count, width = tok_ref.shape
    experts, cap = table_ref.shape
    n_dp, slots, _ = x_ref.shape
    chunks = slots // (experts * MOST)
    cols = width // n_dp
    wait(copies[0])
    table = table_ref[...]
    owner = table // tok_count
    offset = table - owner * tok_count
    mine = (owner == src_ref[0]).astype(F32)
    before = (iota((cap, cap), 0) < iota((cap, cap), 1)).astype(BF16)
    rank = nn(mine.astype(BF16), before)
    col = iota((experts, slots), 1)
    own_col = (col // (MOST * chunks)) == iota((experts, slots), 0)
    col_rank = (col // chunks) % MOST
    wanted = jnp.zeros((1, slots), F32)
    for m in range(MOST):
        chosen = jnp.sum(
            jnp.where(rank == m, mine, 0.0) * (offset + 1).astype(F32), axis=1, keepdims=True
        )
        wanted += jnp.sum(
            jnp.where(own_col & (col_rank == m), chosen, 0.0), axis=0, keepdims=True
        )
    sel = (iota((tok_count, slots), 0) + 1).astype(F32) == wanted
    wait(copies[3])
    wait(copies[1])
    gates = jax.nn.sigmoid(nt(tok_ref[...], router_ref[...]))
    gates_ref[...] = gates
    expand = own_col.astype(BF16)
    gate_exp = sum(nn(p, expand) for p in pieces(gates))
    gsel = jnp.where(sel, gate_exp, 0.0)
    sel_low = sel.astype(BF16)
    sel_ref[...] = sel_low
    gsel_ref[...] = gsel
    start(back)
    ones = jnp.ones((tok_count, LANES), BF16)
    slot_gate = sum(tn(p, ones) for p in pieces(gsel))
    slot_empty = (1.0 - tn(sel_low, ones)) * EMPTY
    chunk = iota((tok_count, slots), 1) % chunks
    pick = jnp.concatenate(
        [jnp.where(chunk == c, sel_low, jnp.zeros_like(sel_low)) for c in range(chunks)], axis=0
    )
    wait(copies[2])
    for d in range(n_dp):
        parts = []
        for c in range(chunks):
            span = slice(d * cols + c * LANES, d * cols + (c + 1) * LANES)
            parts.append(jnp.concatenate([tok_ref[:, span], grad_ref[:, span]], axis=1))
        got = tn(pick, jnp.concatenate(parts, axis=0))
        x_ref[d, :, :LANES] = (got[:, :LANES] + slot_empty).astype(BF16)
        x_ref[d, :, LANES:] = (got[:, LANES:] * slot_gate).astype(BF16)
    wait(back)


def pack_kernel(x_ref, down_ref, p_ref, gated_ref, pick_ref):
    n_dp, rows_all, cols = p_ref.shape
    rows_n = gated_ref.shape[0]
    half = rows_all - rows_n
    cap = rows_n // n_dp
    chunks = cols // LANES
    slots = x_ref.shape[0] // n_dp
    lane = iota((slots, LANES), 1)
    row = iota((slots, LANES), 0)
    held = [x_ref[g * slots : (g + 1) * slots, :LANES] < EMPTY / 2 for g in range(n_dp)]
    a, b = iota((slots, slots), 0), iota((slots, slots), 1)
    before = ((b // chunks < a // chunks) & (b % chunks == 0)).astype(BF16)
    place = nn(before, jnp.concatenate([h.astype(BF16) for h in held], axis=1))
    mine = lane // cap == row % chunks
    want = (lane % cap).astype(F32)
    for g in range(n_dp):
        at = jnp.where(mine, place[:, g * LANES : (g + 1) * LANES], -1.0)
        pick = jnp.where(at == want, held[g].astype(F32), 0.0).astype(BF16)
        pick_ref[g * slots : (g + 1) * slots, :] = pick
        y = tn(pick, x_ref[g * slots : (g + 1) * slots, :]).astype(BF16)
        own = slice(g * cap, (g + 1) * cap)
        for c in range(chunks):
            span = slice(c * LANES, (c + 1) * LANES)
            gated_ref[own, span] = y[c * cap : (c + 1) * cap, LANES:]
            for d in range(n_dp):
                p_ref[d, own, span] = y[c * cap : (c + 1) * cap, :LANES]
    gated = gated_ref[...]
    for d in range(n_dp):
        term = nt(down_ref[2 * d * half : 2 * (d + 1) * half, :], gated).astype(BF16)
        p_ref[d, rows_n:, :rows_n] = term[:half]
        p_ref[d, rows_n:, rows_n:] = term[half:]


def hidden_kernel(src_ref, a_ref, gate_ref, up_ref, router_ref, dh_ref, du_ref, act_ref, lines_ref):
    units, width = gate_ref.shape
    experts = router_ref.shape[0]
    n_dp, rows_all, cols = a_ref.shape
    half = units // 2
    rows_n = rows_all - half
    total = jnp.zeros((2 * units + experts, rows_n), F32)
    dact = jnp.zeros((units, rows_n), F32)
    group = 2
    for d in range(0, n_dp, group):
        span = slice(d * cols, (d + group) * cols)
        left = jnp.concatenate([gate_ref[:, span], up_ref[:, span], router_ref[:, span]], axis=0)
        rows = jnp.concatenate([a_ref[d + i, :rows_n, :] for i in range(group)], axis=1)
        total += nt(left, rows)
    for d in range(n_dp):
        term = a_ref[d, rows_n:, :].astype(F32)
        dact += jnp.concatenate([term[:, :rows_n], term[:, rows_n:]], axis=0)
    h, u, logits = total[:units], total[units : 2 * units], total[2 * units :]
    own = jnp.where(iota(logits.shape, 0) == src_ref[0], logits, 0.0)
    gate = jax.nn.sigmoid(jnp.sum(own, axis=0, keepdims=True))
    sig = jax.nn.sigmoid(h)
    act = (h * sig * u).astype(BF16)
    dh = (dact * u * sig * (1.0 + h * (1.0 - sig))).astype(BF16)
    du = (dact * h * sig).astype(BF16)
    dh_ref[...] = dh
    du_ref[...] = du
    dlogit = jnp.sum(act.astype(F32) * dact, axis=0, keepdims=True) * (1.0 - gate)
    lines = [p.astype(F32) for p in pieces(dlogit)]
    extra = lines_ref.shape[0]
    lines.append(jnp.zeros((extra - len(lines), rows_n), F32))
    lines = jnp.concatenate(lines, axis=0)
    lines_ref[...] = jnp.concatenate([lines, jnp.zeros((extra, cols - rows_n), F32)], axis=1).astype(BF16)
    act_ref[...] = act


def diff_kernel(dh_ref, du_ref, act_ref, lines_ref, gate_ref, up_ref, c_ref):
    units, rows_n = act_ref.shape
    n_dp, _, cols = c_ref.shape
    half = units // 2
    rows_all = rows_n + half
    act, lines = act_ref[...], lines_ref[...]
    dht, dut = dh_ref[...].T, du_ref[...].T
    for d in range(n_dp):
        span = slice(d * cols, (d + 1) * cols)
        c_ref[d, :rows_n, :] = (nn(dht, gate_ref[:, span]) + nn(dut, up_ref[:, span])).astype(BF16)
        c_ref[d, rows_n:rows_all, :rows_n] = act[:half]
        c_ref[d, rows_n:rows_all, rows_n:] = act[half:]
        c_ref[d, rows_all:, :] = lines


def back_kernel(c_ref, a_ref, down_ref, pick_ref, z_out, r_ref, act_out, z_ref, act_ref, sem):
    n_dp, rows_all, cols = a_ref.shape
    half = act_ref.shape[0] // (2 * n_dp)
    rows_n = rows_all - half
    cap = rows_n // n_dp
    chunks = cols // LANES
    slots = z_ref.shape[0] // n_dp
    diff = jnp.zeros((rows_n, cols), F32)
    packed = jnp.zeros((c_ref.shape[1] - rows_all, cols), F32)
    for d in range(n_dp):
        act_ref[2 * d * half : (2 * d + 1) * half, :] = c_ref[d, rows_n:rows_all, :rows_n]
        act_ref[(2 * d + 1) * half : 2 * (d + 1) * half, :] = c_ref[d, rows_n:rows_all, rows_n:]
        diff += c_ref[d, :rows_n, :].astype(F32)
        packed += c_ref[d, rows_all:, :].astype(F32)
    copies = [pltpu.make_async_copy(act_ref, act_out, sem.at[n_dp])]
    copies[0].start()
    diff = diff.astype(BF16)
    out = tn(act_ref[...], down_ref[...]).astype(BF16)
    for g in range(n_dp):
        own = slice(g * cap, (g + 1) * cap)
        y = jnp.concatenate(
            [
                jnp.concatenate([x[own, c * LANES : (c + 1) * LANES] for x in (out, diff)], axis=1)
                for c in range(chunks)
            ],
            axis=0,
        )
        at = slice(g * slots, (g + 1) * slots)
        z_ref[at, :] = nn(pick_ref[at, :], y).astype(BF16)
        copies.append(pltpu.make_async_copy(z_ref.at[at], z_out.at[at], sem.at[g]))
        copies[-1].start()
    dlogit = packed[:1, :rows_n] + packed[1:2, :rows_n] + packed[2:3, :rows_n]
    terms = [p.astype(F32) for p in pieces(dlogit)]
    terms = jnp.concatenate(terms + [jnp.zeros((8 - len(terms), rows_n), F32)], axis=0).astype(BF16)
    part = r_ref.shape[1]
    lines = []
    for d in range(n_dp):
        line = jnp.sum(nn(terms, a_ref[d, :rows_n, :]), axis=0, keepdims=True)
        lines += [line[:, i : i + part] for i in range(0, cols, part)]
    r_ref[...] = jnp.concatenate(lines, axis=0).astype(BF16)
    for copy in copies:
        copy.wait()


def weight_kernel(dh_ref, du_ref, act_ref, gated_ref, a_ref, gg_ref, ug_ref, dg_ref):
    n_dp, _, cols = a_ref.shape
    rows_n = gated_ref.shape[0]
    dh, du, gated = dh_ref[...], du_ref[...], gated_ref[...]
    for d in range(n_dp):
        span = slice(d * cols, (d + 1) * cols)
        rows = a_ref[d, :rows_n, :]
        gg_ref[:, span] = nn(dh, rows).astype(BF16)
        ug_ref[:, span] = nn(du, rows).astype(BF16)
    step = 256
    for j in range(0, dg_ref.shape[0], step):
        dg_ref[j : j + step, :] = nn(act_ref[j : j + step, :], gated).astype(BF16)


def take_kernel(src_ref, r_ref, *refs):
    far, outs_far, near, near_out, sem = refs[:6], refs[6:9], refs[9:15], refs[15:18], refs[18]
    d_ref, sel_ref, gsel_ref, gates_ref, grad_ref, router_ref = near
    mixed_ref, tgrad_ref, rgrad_ref = near_out
    copies, at = [], 0
    for a, b, n in zip(far, near, (4, 1, 1, 1, 1, 1)):
        copies.append(chunked(a, b, n, sem, at))
        at += n
    for i in (1, 2, 0, 4, 3, 5):
        start(copies[i])
    tok_count, width = grad_ref.shape
    experts = gates_ref.shape[1]
    slots = sel_ref.shape[1]
    n_dp = d_ref.shape[0] // slots
    chunks = slots // (experts * MOST)
    cols = width // n_dp
    rgrad_back = chunked(rgrad_ref, outs_far[2], 1, sem, at)
    at += 1

    def column_copies(i, at):
        blocks = [pl.ds(d * cols, 2 * cols) for d in range(0, n_dp, 2)]
        return [
            pltpu.make_async_copy(near_out[i].at[:, b], outs_far[i].at[:, b], sem.at[at + d])
            for d, b in enumerate(blocks)
        ]

    mixed_back = column_copies(0, at)
    tgrad_back = column_copies(1, at + n_dp)
    chunk = iota((tok_count, slots), 1) % chunks

    def by_chunk(x):
        return jnp.concatenate(
            [jnp.where(chunk == c, x, jnp.zeros_like(x)) for c in range(chunks)], axis=0
        )

    def span(d, c):
        return slice(d * cols + c * LANES, d * cols + (c + 1) * LANES)

    def both(d, lanes):
        return jnp.concatenate(
            [d_ref[i * slots : (i + 1) * slots, lanes] for i in (d, d + 1)], axis=1
        )

    wait(copies[1])
    wait(copies[2])
    pick = by_chunk(sel_ref[...])
    weights = [by_chunk(w) for w in pieces(gsel_ref[...])]
    hits = jnp.zeros(pick.shape, F32)
    for d in range(0, n_dp, 2):
        wait(copies[0][d // 2 : d // 2 + 1])
        outs = both(d, slice(0, LANES))
        mixed = sum(nn(w, outs) for w in weights).astype(BF16)
        for i in range(2):
            for c in range(chunks):
                mixed_ref[:, span(d + i, c)] = mixed[
                    c * tok_count : (c + 1) * tok_count, i * LANES : (i + 1) * LANES
                ]
        mixed_back[d // 2].start()
        if d == 0:
            wait(copies[4])
        grads = jnp.concatenate(
            [
                jnp.concatenate([grad_ref[:, span(d + i, c)] for i in range(2)], axis=1)
                for c in range(chunks)
            ],
            axis=0,
        )
        hits += nt(grads, outs)
    n_rows, part = r_ref.shape
    lines = n_rows // experts
    me = src_ref[0]
    me_x, me_z, me_c = me // 8, (me // 2) % 4, me % 2
    row, col = iota((n_rows, n_rows), 0), iota((n_rows, n_rows), 1)
    block = col // lines
    source = ((me_x + 4 - (block // 2) % 4) % 4) * 8 + ((me_z + 4 - block // 8) % 4) * 2 + (me_c + block) % 2
    sort = ((row % experts == source) & (row // experts == col % lines)).astype(BF16)
    rgrad = nn(sort, r_ref[...])
    for i in range(lines):
        rgrad_ref[:, i * part : (i + 1) * part] = rgrad[i * experts : (i + 1) * experts]
    start(rgrad_back)
    hits = jnp.where(pick != 0, hits, 0.0)
    hits = sum(hits[c * tok_count : (c + 1) * tok_count] for c in range(chunks))
    collect = (iota((slots, experts), 0) // (MOST * chunks) == iota((slots, experts), 1)).astype(BF16)
    wait(copies[3])
    wait(copies[5])
    gates = gates_ref[...]
    dlogit = sum(nn(p, collect) for p in pieces(hits)) * gates * (1.0 - gates)
    terms = jnp.concatenate(pieces(dlogit), axis=1)
    for d in range(0, n_dp, 2):
        diffs = nn(pick, both(d, slice(LANES, 2 * LANES)))
        router = router_ref[:, d * cols : (d + 2) * cols]
        from_router = nn(terms, jnp.concatenate([router] * 3, axis=0))
        for i in range(2):
            for c in range(chunks):
                at = i * cols + c * LANES
                tgrad_ref[:, span(d + i, c)] = (
                    diffs[c * tok_count : (c + 1) * tok_count, i * LANES : (i + 1) * LANES]
                    + from_router[:, at : at + LANES]
                ).astype(BF16)
        tgrad_back[d // 2].start()
    wait(rgrad_back)
    wait(mixed_back)
    wait(tgrad_back)


def spread(r):
    def shifted(x, k, to):
        return lax.ppermute(x, "expert", [(e, to(e, k)) for e in range(32)])

    def core(e, k):
        return e // 2 * 2 + (e + k) % 2

    def along_x(e, k):
        return (e + 8 * k) % 32

    def along_z(e, k):
        return e // 8 * 8 + (e + 2 * k) % 8

    for to, n in ((core, 2), (along_x, 4), (along_z, 4)):
        half = r
        r = jnp.concatenate([r] + [shifted(r, k, to) for k in range(1, n)], axis=0)
    return r, half


def local(tokens, out_grad, router, choice_index, gate_weight, up_weight, down_weight):
    tok, grad, table = tokens[0], out_grad[0], choice_index[0]
    gate, up, down = gate_weight[0], up_weight[0], down_weight[0]
    router = router.T
    tok_count, width = tok.shape
    experts, cap = table.shape
    units, cols = gate.shape[0], down.shape[1]
    n_dp = lax.axis_size("dp")
    rows_n = n_dp * cap
    chunks = cols // LANES
    per = MOST * chunks
    slots = experts * per
    rows_all = rows_n + units // 2
    src = lax.axis_index("expert").astype(jnp.int32).reshape(1)

    def swap(x, axis):
        return lax.all_to_all(x, axis, split_axis=0, concat_axis=0, tiled=True)

    kept = [((tok_count, slots), BF16), ((tok_count, slots), F32), ((tok_count, experts), F32)]
    x, sel, gsel, gates = call(
        send_kernel,
        [((n_dp, slots, 2 * LANES), BF16)] + kept,
        (src, table, tok, grad, router),
        far_in=(1, 2, 3, 4),
        far_out=(1, 2, 3),
        scratch=[pltpu.VMEM(a.shape, a.dtype) for a in (table, tok, grad, router)]
        + [pltpu.VMEM(s, d) for s, d in kept]
        + [pltpu.SemaphoreType.DMA((11 + len(kept),))],
    )
    x = swap(x.reshape(n_dp * experts, per, 2 * LANES), ("dp", "expert"))
    a, gated, pick = call(
        pack_kernel,
        [
            ((n_dp, rows_all, cols), BF16),
            ((rows_n, cols), BF16),
            ((n_dp * slots, LANES), BF16),
        ],
        (x.reshape(n_dp * slots, 2 * LANES), down),
    )
    a = swap(a, "dp")
    dh, du, act, lines = call(
        hidden_kernel,
        [((units, rows_n), BF16)] * 3 + [((16, cols), BF16)],
        (src, a, gate, up, router),
    )
    (c,) = call(
        diff_kernel, [((n_dp, rows_all + 16, cols), BF16)], (dh, du, act, lines, gate, up)
    )
    c = swap(c, "dp")
    z, r, act = call(
        back_kernel,
        [
            ((n_dp * slots, 2 * LANES), BF16),
            ((16, width // 16), BF16),
            ((n_dp * units, rows_n), BF16),
        ],
        (c, a, down, pick),
        far_out=(0, 2),
        scratch=[
            pltpu.VMEM((n_dp * slots, 2 * LANES), BF16),
            pltpu.VMEM((n_dp * units, rows_n), BF16),
            pltpu.SemaphoreType.DMA((n_dp + 1,)),
        ],
    )
    z = swap(z.reshape(n_dp * experts, per, 2 * LANES), ("dp", "expert"))
    r, half = spread(r)
    dh, half = lax.optimization_barrier((dh, half))
    gate_grad, up_grad, down_grad = call(
        weight_kernel,
        [((units, width), BF16), ((units, width), BF16), ((n_dp * units, cols), BF16)],
        (dh, du, act, gated, a),
    )
    taken = (z.reshape(n_dp * slots, 2 * LANES), sel, gsel, gates, grad, router)
    results = [((tok_count, width), BF16), ((tok_count, width), BF16), ((experts, width), F32)]
    mixed, token_grad, router_grad = call(
        take_kernel,
        results,
        (src, r) + taken,
        far_in=range(2, 8),
        far_out=range(3),
        scratch=[pltpu.VMEM(a.shape, a.dtype) for a in taken]
        + [pltpu.VMEM(s, d) for s, d in results]
        + [pltpu.SemaphoreType.DMA((21 + 2 * n_dp,))],
    )
    return (
        mixed[None],
        token_grad[None],
        router_grad.T,
        gate_grad[None],
        up_grad[None],
        down_grad[None],
    )


def solution(mesh):
    in_specs = (
        P("dp", "expert", None),
        P("dp", "expert", None),
        P(),
        P("dp", None, None),
        P("expert", "dp", None),
        P("expert", "dp", None),
        P("expert", None, "dp"),
    )
    out_specs = (
        P("dp", "expert", None),
        P("dp", "expert", None),
        P(),
        P("expert", "dp", None),
        P("expert", "dp", None),
        P("expert", None, "dp"),
    )
    return jax.shard_map(local, mesh=mesh, in_specs=in_specs, out_specs=out_specs, check_vma=False)
```

```python
import jax
import jax.numpy as jnp
from jax import lax
from jax.experimental import pallas as pl
from jax.experimental.pallas import tpu as pltpu
from jax.sharding import PartitionSpec as P

MOST = 2
LANES = 128
EMPTY = 1024.0
F32 = jnp.float32
BF16 = jnp.bfloat16
VMEM = pl.BlockSpec(memory_space=pltpu.VMEM)
SMEM = pl.BlockSpec(memory_space=pltpu.SMEM)
FAR = pl.BlockSpec(memory_space=pltpu.HBM)


def iota(shape, dim):
    return lax.broadcasted_iota(jnp.int32, shape, dim)


def nn(a, b):
    return lax.dot_general(a, b, (((1,), (0,)), ((), ())), preferred_element_type=F32)


def nt(a, b):
    return lax.dot_general(a, b, (((1,), (1,)), ((), ())), preferred_element_type=F32)


def tn(a, b):
    return lax.dot_general(a, b, (((0,), (0,)), ((), ())), preferred_element_type=F32)


def pieces(x):
    hi = x.astype(BF16)
    return hi, (x - hi.astype(F32)).astype(BF16)


def call(kernel, outs, args, far_in=(), far_out=(), scratch=()):
    args = [
        pltpu.with_memory_space_constraint(a, pltpu.HBM) if i in far_in else a for i, a in enumerate(args)
    ]
    return pl.pallas_call(
        kernel,
        out_shape=tuple(
            pltpu.HBM(s, d) if i in far_out else jax.ShapeDtypeStruct(s, d)
            for i, (s, d) in enumerate(outs)
        ),
        in_specs=[SMEM if a.ndim == 1 else FAR if i in far_in else VMEM for i, a in enumerate(args)],
        out_specs=tuple(FAR if i in far_out else VMEM for i in range(len(outs))),
        scratch_shapes=scratch,
        compiler_params=pltpu.CompilerParams(vmem_limit_bytes=40 * 2**20),
    )(*args)


def chunked(src, dst, n, sem, at):
    rows = src.shape[0] // n
    parts = [pl.ds(i * rows, rows) for i in range(n)]
    return [pltpu.make_async_copy(src.at[p], dst.at[p], sem.at[at + i]) for i, p in enumerate(parts)]


def start(copies):
    for copy in copies:
        copy.start()


def wait(copies):
    for copy in copies:
        copy.wait()


def send_kernel(src_ref, *refs):
    far, x_ref, outs_far, near, near_out, sem = refs[:4], refs[4], refs[5:8], refs[8:12], refs[12:15], refs[15]
    sel_ref, gsel_ref, gates_ref = near_out
    copies, at = [], 0
    for src, dst, n in zip(far, near, (1, 4, 4, 2)):
        copies.append(chunked(src, dst, n, sem, at))
        at += n
    back = [pltpu.make_async_copy(a, b, sem.at[at + i]) for i, (a, b) in enumerate(zip(near_out, outs_far))]
    for i in (0, 3, 1, 2):
        start(copies[i])
    table_ref, tok_ref, grad_ref, router_ref = near
    tok_count, width = tok_ref.shape
    experts, cap = table_ref.shape
    n_dp, slots, _ = x_ref.shape
    chunks = slots // (experts * MOST)
    cols = width // n_dp
    wait(copies[0])
    table = table_ref[...]
    owner = table // tok_count
    offset = table - owner * tok_count
    mine = (owner == src_ref[0]).astype(F32)
    before = (iota((cap, cap), 0) < iota((cap, cap), 1)).astype(BF16)
    rank = nn(mine.astype(BF16), before)
    col = iota((experts, slots), 1)
    own_col = (col // (MOST * chunks)) == iota((experts, slots), 0)
    col_rank = (col // chunks) % MOST
    wanted = jnp.zeros((1, slots), F32)
    for m in range(MOST):
        chosen = jnp.sum(
            jnp.where(rank == m, mine, 0.0) * (offset + 1).astype(F32), axis=1, keepdims=True
        )
        wanted += jnp.sum(
            jnp.where(own_col & (col_rank == m), chosen, 0.0), axis=0, keepdims=True
        )
    sel = (iota((tok_count, slots), 0) + 1).astype(F32) == wanted
    wait(copies[3])
    wait(copies[1])
    gates = jax.nn.sigmoid(nt(tok_ref[...], router_ref[...]))
    gates_ref[...] = gates
    expand = own_col.astype(BF16)
    gate_exp = sum(nn(p, expand) for p in pieces(gates))
    gsel = jnp.where(sel, gate_exp, 0.0)
    sel_low = sel.astype(BF16)
    sel_ref[...] = sel_low
    gsel_ref[...] = gsel
    start(back)
    ones = jnp.ones((tok_count, LANES), BF16)
    slot_gate = sum(tn(p, ones) for p in pieces(gsel))
    slot_empty = (1.0 - tn(sel_low, ones)) * EMPTY
    chunk = iota((tok_count, slots), 1) % chunks
    pick = jnp.concatenate(
        [jnp.where(chunk == c, sel_low, jnp.zeros_like(sel_low)) for c in range(chunks)], axis=0
    )
    wait(copies[2])
    for d in range(n_dp):
        parts = []
        for c in range(chunks):
            span = slice(d * cols + c * LANES, d * cols + (c + 1) * LANES)
            parts.append(jnp.concatenate([tok_ref[:, span], grad_ref[:, span]], axis=1))
        got = tn(pick, jnp.concatenate(parts, axis=0))
        x_ref[d, :, :LANES] = (got[:, :LANES] + slot_empty).astype(BF16)
        x_ref[d, :, LANES:] = (got[:, LANES:] * slot_gate).astype(BF16)
    wait(back)


def pack_kernel(x_ref, down_ref, p_ref, gated_ref, pick_ref):
    n_dp, rows_all, cols = p_ref.shape
    rows_n = gated_ref.shape[0]
    half = rows_all - rows_n
    cap = rows_n // n_dp
    chunks = cols // LANES
    slots = x_ref.shape[0] // n_dp
    lane = iota((slots, LANES), 1)
    row = iota((slots, LANES), 0)
    held = [x_ref[g * slots : (g + 1) * slots, :LANES] < EMPTY / 2 for g in range(n_dp)]
    a, b = iota((slots, slots), 0), iota((slots, slots), 1)
    before = ((b // chunks < a // chunks) & (b % chunks == 0)).astype(BF16)
    place = nn(before, jnp.concatenate([h.astype(BF16) for h in held], axis=1))
    mine = lane // cap == row % chunks
    want = (lane % cap).astype(F32)
    for g in range(n_dp):
        at = jnp.where(mine, place[:, g * LANES : (g + 1) * LANES], -1.0)
        pick = jnp.where(at == want, held[g].astype(F32), 0.0).astype(BF16)
        pick_ref[g * slots : (g + 1) * slots, :] = pick
        y = tn(pick, x_ref[g * slots : (g + 1) * slots, :]).astype(BF16)
        own = slice(g * cap, (g + 1) * cap)
        for c in range(chunks):
            span = slice(c * LANES, (c + 1) * LANES)
            gated_ref[own, span] = y[c * cap : (c + 1) * cap, LANES:]
            for d in range(n_dp):
                p_ref[d, own, span] = y[c * cap : (c + 1) * cap, :LANES]
    gated = gated_ref[...]
    for d in range(n_dp):
        term = nt(down_ref[2 * d * half : 2 * (d + 1) * half, :], gated).astype(BF16)
        p_ref[d, rows_n:, :rows_n] = term[:half]
        p_ref[d, rows_n:, rows_n:] = term[half:]


def hidden_kernel(src_ref, a_ref, gate_ref, up_ref, router_ref, dh_ref, du_ref, act_ref, lines_ref):
    units, width = gate_ref.shape
    experts = router_ref.shape[0]
    n_dp, rows_all, cols = a_ref.shape
    half = units // 2
    rows_n = rows_all - half
    total = jnp.zeros((2 * units + experts, rows_n), F32)
    dact = jnp.zeros((units, rows_n), F32)
    group = 2
    for d in range(0, n_dp, group):
        span = slice(d * cols, (d + group) * cols)
        left = jnp.concatenate([gate_ref[:, span], up_ref[:, span], router_ref[:, span]], axis=0)
        rows = jnp.concatenate([a_ref[d + i, :rows_n, :] for i in range(group)], axis=1)
        total += nt(left, rows)
    for d in range(n_dp):
        term = a_ref[d, rows_n:, :].astype(F32)
        dact += jnp.concatenate([term[:, :rows_n], term[:, rows_n:]], axis=0)
    h, u, logits = total[:units], total[units : 2 * units], total[2 * units :]
    own = jnp.where(iota(logits.shape, 0) == src_ref[0], logits, 0.0)
    gate = jax.nn.sigmoid(jnp.sum(own, axis=0, keepdims=True))
    sig = jax.nn.sigmoid(h)
    act = (h * sig * u).astype(BF16)
    dh = (dact * u * sig * (1.0 + h * (1.0 - sig))).astype(BF16)
    du = (dact * h * sig).astype(BF16)
    dh_ref[...] = dh
    du_ref[...] = du
    dlogit = jnp.sum(act.astype(F32) * dact, axis=0, keepdims=True) * (1.0 - gate)
    lines = [p.astype(F32) for p in pieces(dlogit)]
    extra = lines_ref.shape[0]
    lines.append(jnp.zeros((extra - len(lines), rows_n), F32))
    lines = jnp.concatenate(lines, axis=0)
    lines_ref[...] = jnp.concatenate([lines, jnp.zeros((extra, cols - rows_n), F32)], axis=1).astype(BF16)
    act_ref[...] = act


def diff_kernel(dh_ref, du_ref, act_ref, lines_ref, gate_ref, up_ref, c_ref):
    units, rows_n = act_ref.shape
    n_dp, _, cols = c_ref.shape
    half = units // 2
    rows_all = rows_n + half
    act, lines = act_ref[...], lines_ref[...]
    dht, dut = dh_ref[...].T, du_ref[...].T
    for d in range(n_dp):
        span = slice(d * cols, (d + 1) * cols)
        c_ref[d, :rows_n, :] = (nn(dht, gate_ref[:, span]) + nn(dut, up_ref[:, span])).astype(BF16)
        c_ref[d, rows_n:rows_all, :rows_n] = act[:half]
        c_ref[d, rows_n:rows_all, rows_n:] = act[half:]
        c_ref[d, rows_all:, :] = lines


def back_kernel(c_ref, a_ref, down_ref, pick_ref, z_out, r_ref, act_out, z_ref, act_ref, sem):
    n_dp, rows_all, cols = a_ref.shape
    half = act_ref.shape[0] // (2 * n_dp)
    rows_n = rows_all - half
    cap = rows_n // n_dp
    chunks = cols // LANES
    slots = z_ref.shape[0] // n_dp
    diff = jnp.zeros((rows_n, cols), F32)
    packed = jnp.zeros((c_ref.shape[1] - rows_all, cols), F32)
    for d in range(n_dp):
        act_ref[2 * d * half : (2 * d + 1) * half, :] = c_ref[d, rows_n:rows_all, :rows_n]
        act_ref[(2 * d + 1) * half : 2 * (d + 1) * half, :] = c_ref[d, rows_n:rows_all, rows_n:]
        diff += c_ref[d, :rows_n, :].astype(F32)
        packed += c_ref[d, rows_all:, :].astype(F32)
    copies = [pltpu.make_async_copy(act_ref, act_out, sem.at[n_dp])]
    copies[0].start()
    diff = diff.astype(BF16)
    out = tn(act_ref[...], down_ref[...]).astype(BF16)
    for g in range(n_dp):
        own = slice(g * cap, (g + 1) * cap)
        y = jnp.concatenate(
            [
                jnp.concatenate([x[own, c * LANES : (c + 1) * LANES] for x in (out, diff)], axis=1)
                for c in range(chunks)
            ],
            axis=0,
        )
        at = slice(g * slots, (g + 1) * slots)
        z_ref[at, :] = nn(pick_ref[at, :], y).astype(BF16)
        copies.append(pltpu.make_async_copy(z_ref.at[at], z_out.at[at], sem.at[g]))
        copies[-1].start()
    dlogit = packed[:1, :rows_n] + packed[1:2, :rows_n]
    terms = [p.astype(F32) for p in pieces(dlogit)]
    terms = jnp.concatenate(terms + [jnp.zeros((8 - len(terms), rows_n), F32)], axis=0).astype(BF16)
    part = r_ref.shape[1]
    lines = []
    for d in range(n_dp):
        line = jnp.sum(nn(terms, a_ref[d, :rows_n, :]), axis=0, keepdims=True)
        lines += [line[:, i : i + part] for i in range(0, cols, part)]
    r_ref[...] = jnp.concatenate(lines, axis=0).astype(BF16)
    for copy in copies:
        copy.wait()


def weight_kernel(dh_ref, du_ref, act_ref, gated_ref, a_ref, gg_ref, ug_ref, dg_ref):
    n_dp, _, cols = a_ref.shape
    rows_n = gated_ref.shape[0]
    dh, du, gated = dh_ref[...], du_ref[...], gated_ref[...]
    for d in range(n_dp):
        span = slice(d * cols, (d + 1) * cols)
        rows = a_ref[d, :rows_n, :]
        gg_ref[:, span] = nn(dh, rows).astype(BF16)
        ug_ref[:, span] = nn(du, rows).astype(BF16)
    step = 256
    for j in range(0, dg_ref.shape[0], step):
        dg_ref[j : j + step, :] = nn(act_ref[j : j + step, :], gated).astype(BF16)


def take_kernel(src_ref, r_ref, *refs):
    far, outs_far, near, near_out, sem = refs[:6], refs[6:9], refs[9:15], refs[15:18], refs[18]
    d_ref, sel_ref, gsel_ref, gates_ref, grad_ref, router_ref = near
    mixed_ref, tgrad_ref, rgrad_ref = near_out
    copies, at = [], 0
    for a, b, n in zip(far, near, (4, 1, 1, 1, 1, 1)):
        copies.append(chunked(a, b, n, sem, at))
        at += n
    for i in (1, 2, 0, 4, 3, 5):
        start(copies[i])
    tok_count, width = grad_ref.shape
    experts = gates_ref.shape[1]
    slots = sel_ref.shape[1]
    n_dp = d_ref.shape[0] // slots
    chunks = slots // (experts * MOST)
    cols = width // n_dp
    rgrad_back = chunked(rgrad_ref, outs_far[2], 1, sem, at)
    at += 1

    def column_copies(i, at):
        blocks = [pl.ds(d * cols, 2 * cols) for d in range(0, n_dp, 2)]
        return [
            pltpu.make_async_copy(near_out[i].at[:, b], outs_far[i].at[:, b], sem.at[at + d])
            for d, b in enumerate(blocks)
        ]

    mixed_back = column_copies(0, at)
    tgrad_back = column_copies(1, at + n_dp)
    chunk = iota((tok_count, slots), 1) % chunks

    def by_chunk(x):
        return jnp.concatenate(
            [jnp.where(chunk == c, x, jnp.zeros_like(x)) for c in range(chunks)], axis=0
        )

    def span(d, c):
        return slice(d * cols + c * LANES, d * cols + (c + 1) * LANES)

    def both(d, lanes):
        return jnp.concatenate(
            [d_ref[i * slots : (i + 1) * slots, lanes] for i in (d, d + 1)], axis=1
        )

    wait(copies[1])
    wait(copies[2])
    pick = by_chunk(sel_ref[...])
    weights = [by_chunk(w) for w in pieces(gsel_ref[...])]
    hits = jnp.zeros(pick.shape, F32)
    for d in range(0, n_dp, 2):
        wait(copies[0][d // 2 : d // 2 + 1])
        outs = both(d, slice(0, LANES))
        mixed = sum(nn(w, outs) for w in weights).astype(BF16)
        for i in range(2):
            for c in range(chunks):
                mixed_ref[:, span(d + i, c)] = mixed[
                    c * tok_count : (c + 1) * tok_count, i * LANES : (i + 1) * LANES
                ]
        mixed_back[d // 2].start()
        if d == 0:
            wait(copies[4])
        grads = jnp.concatenate(
            [
                jnp.concatenate([grad_ref[:, span(d + i, c)] for i in range(2)], axis=1)
                for c in range(chunks)
            ],
            axis=0,
        )
        hits += nt(grads, outs)
    n_rows, part = r_ref.shape
    lines = n_rows // experts
    me = src_ref[0]
    me_x, me_z = me // 8, (me // 2) % 4
    row, col = iota((n_rows, n_rows), 0), iota((n_rows, n_rows), 1)
    block = col // lines
    source = ((me_x + 4 - (block // 2) % 4) % 4) * 8 + ((me_z + 4 - block // 8) % 4) * 2 + block % 2
    sort = ((row % experts == source) & (row // experts == col % lines)).astype(BF16)
    rgrad = nn(sort, r_ref[...])
    for i in range(lines):
        rgrad_ref[:, i * part : (i + 1) * part] = rgrad[i * experts : (i + 1) * experts]
    start(rgrad_back)
    hits = jnp.where(pick != 0, hits, 0.0)
    hits = sum(hits[c * tok_count : (c + 1) * tok_count] for c in range(chunks))
    collect = (iota((slots, experts), 0) // (MOST * chunks) == iota((slots, experts), 1)).astype(BF16)
    wait(copies[3])
    wait(copies[5])
    gates = gates_ref[...]
    dlogit = sum(nn(p, collect) for p in pieces(hits)) * gates * (1.0 - gates)
    terms = jnp.concatenate(pieces(dlogit), axis=1)
    for d in range(0, n_dp, 2):
        diffs = nn(pick, both(d, slice(LANES, 2 * LANES)))
        router = router_ref[:, d * cols : (d + 2) * cols]
        from_router = nn(terms, jnp.concatenate([router] * 2, axis=0))
        for i in range(2):
            for c in range(chunks):
                at = i * cols + c * LANES
                tgrad_ref[:, span(d + i, c)] = (
                    diffs[c * tok_count : (c + 1) * tok_count, i * LANES : (i + 1) * LANES]
                    + from_router[:, at : at + LANES]
                ).astype(BF16)
        tgrad_back[d // 2].start()
    wait(rgrad_back)
    wait(mixed_back)
    wait(tgrad_back)


def shifted(x, k, to):
    return lax.ppermute(x, "expert", [(e, to(e, k)) for e in range(32)])


def paired(x, axis):
    got = shifted(x, 1, lambda e, k: e ^ k)
    first = lax.axis_index("expert") % 2 == 0
    return jnp.where(first, jnp.concatenate([x, got], axis), jnp.concatenate([got, x], axis))


def spread(r):
    def along_x(e, k):
        return (e + 8 * k) % 32

    def along_z(e, k):
        return e // 8 * 8 + (e + 2 * k) % 8

    r = paired(r, 0)
    r = jnp.concatenate([r] + [shifted(r, k, along_x) for k in range(1, 4)], axis=0)
    middle = r.shape[1] // 2
    half = jnp.where(lax.axis_index("expert") % 2 == 0, r[:, :middle], r[:, middle:])
    return jnp.concatenate([half] + [shifted(half, k, along_z) for k in range(1, 4)], axis=0)


def local(tokens, out_grad, router, choice_index, gate_weight, up_weight, down_weight):
    tok, grad, table = tokens[0], out_grad[0], choice_index[0]
    gate, up, down = gate_weight[0], up_weight[0], down_weight[0]
    router = router.T
    tok_count, width = tok.shape
    experts, cap = table.shape
    units, cols = gate.shape[0], down.shape[1]
    n_dp = lax.axis_size("dp")
    rows_n = n_dp * cap
    chunks = cols // LANES
    per = MOST * chunks
    slots = experts * per
    rows_all = rows_n + units // 2
    src = lax.axis_index("expert").astype(jnp.int32).reshape(1)

    def swap(x, axis):
        return lax.all_to_all(x, axis, split_axis=0, concat_axis=0, tiled=True)

    kept = [((tok_count, slots), BF16), ((tok_count, slots), F32), ((tok_count, experts), F32)]
    x, sel, gsel, gates = call(
        send_kernel,
        [((n_dp, slots, 2 * LANES), BF16)] + kept,
        (src, table, tok, grad, router),
        far_in=(1, 2, 3, 4),
        far_out=(1, 2, 3),
        scratch=[pltpu.VMEM(a.shape, a.dtype) for a in (table, tok, grad, router)]
        + [pltpu.VMEM(s, d) for s, d in kept]
        + [pltpu.SemaphoreType.DMA((11 + len(kept),))],
    )
    x = swap(x.reshape(n_dp * experts, per, 2 * LANES), ("dp", "expert"))
    a, gated, pick = call(
        pack_kernel,
        [
            ((n_dp, rows_all, cols), BF16),
            ((rows_n, cols), BF16),
            ((n_dp * slots, LANES), BF16),
        ],
        (x.reshape(n_dp * slots, 2 * LANES), down),
    )
    a = swap(a, "dp")
    dh, du, act, lines = call(
        hidden_kernel,
        [((units, rows_n), BF16)] * 3 + [((16, cols), BF16)],
        (src, a, gate, up, router),
    )
    (c,) = call(
        diff_kernel, [((n_dp, rows_all + 16, cols), BF16)], (dh, du, act, lines, gate, up)
    )
    c = swap(c, "dp")
    z, r, act = call(
        back_kernel,
        [
            ((n_dp * slots, 2 * LANES), BF16),
            ((16, width // 16), BF16),
            ((n_dp * units, rows_n), BF16),
        ],
        (c, a, down, pick),
        far_out=(0, 2),
        scratch=[
            pltpu.VMEM((n_dp * slots, 2 * LANES), BF16),
            pltpu.VMEM((n_dp * units, rows_n), BF16),
            pltpu.SemaphoreType.DMA((n_dp + 1,)),
        ],
    )
    z = swap(z.reshape(n_dp * experts, per, 2 * LANES), ("dp", "expert"))
    r = spread(r)
    gate_grad, up_grad, down_grad = call(
        weight_kernel,
        [((units, width), BF16), ((units, width), BF16), ((n_dp * units, cols), BF16)],
        (dh, du, act, gated, a),
    )
    taken = (z.reshape(n_dp * slots, 2 * LANES), sel, gsel, gates, grad, router)
    r, gate_grad, up_grad, down_grad = lax.optimization_barrier((r, gate_grad, up_grad, down_grad))
    r = paired(r, 1)
    results = [((tok_count, width), BF16), ((tok_count, width), BF16), ((experts, width), F32)]
    mixed, token_grad, router_grad = call(
        take_kernel,
        results,
        (src, r) + taken,
        far_in=range(2, 8),
        far_out=range(3),
        scratch=[pltpu.VMEM(a.shape, a.dtype) for a in taken]
        + [pltpu.VMEM(s, d) for s, d in results]
        + [pltpu.SemaphoreType.DMA((21 + 2 * n_dp,))],
    )
    return (
        mixed[None],
        token_grad[None],
        router_grad.T,
        gate_grad[None],
        up_grad[None],
        down_grad[None],
    )


def solution(mesh):
    in_specs = (
        P("dp", "expert", None),
        P("dp", "expert", None),
        P(),
        P("dp", None, None),
        P("expert", "dp", None),
        P("expert", "dp", None),
        P("expert", None, "dp"),
    )
    out_specs = (
        P("dp", "expert", None),
        P("dp", "expert", None),
        P(),
        P("expert", "dp", None),
        P("expert", "dp", None),
        P("expert", None, "dp"),
    )
    return jax.shard_map(local, mesh=mesh, in_specs=in_specs, out_specs=out_specs, check_vma=False)
```

```python
import jax
import jax.numpy as jnp
from jax import lax
from jax.experimental import pallas as pl
from jax.experimental.pallas import tpu as pltpu
from jax.sharding import PartitionSpec as P

MOST = 2
LANES = 128
EMPTY = 1024.0
F32 = jnp.float32
BF16 = jnp.bfloat16
VMEM = pl.BlockSpec(memory_space=pltpu.VMEM)
SMEM = pl.BlockSpec(memory_space=pltpu.SMEM)
FAR = pl.BlockSpec(memory_space=pltpu.HBM)


def iota(shape, dim):
    return lax.broadcasted_iota(jnp.int32, shape, dim)


def nn(a, b):
    return lax.dot_general(a, b, (((1,), (0,)), ((), ())), preferred_element_type=F32)


def nt(a, b):
    return lax.dot_general(a, b, (((1,), (1,)), ((), ())), preferred_element_type=F32)


def tn(a, b):
    return lax.dot_general(a, b, (((0,), (0,)), ((), ())), preferred_element_type=F32)


def pieces(x):
    hi = x.astype(BF16)
    return hi, (x - hi.astype(F32)).astype(BF16)


def call(kernel, outs, args, far_in=(), far_out=(), scratch=()):
    args = [
        pltpu.with_memory_space_constraint(a, pltpu.HBM) if i in far_in else a for i, a in enumerate(args)
    ]
    return pl.pallas_call(
        kernel,
        out_shape=tuple(
            pltpu.HBM(s, d) if i in far_out else jax.ShapeDtypeStruct(s, d)
            for i, (s, d) in enumerate(outs)
        ),
        in_specs=[SMEM if a.ndim == 1 else FAR if i in far_in else VMEM for i, a in enumerate(args)],
        out_specs=tuple(FAR if i in far_out else VMEM for i in range(len(outs))),
        scratch_shapes=scratch,
        compiler_params=pltpu.CompilerParams(vmem_limit_bytes=40 * 2**20),
    )(*args)


def chunked(src, dst, n, sem, at):
    rows = src.shape[0] // n
    parts = [pl.ds(i * rows, rows) for i in range(n)]
    return [pltpu.make_async_copy(src.at[p], dst.at[p], sem.at[at + i]) for i, p in enumerate(parts)]


def start(copies):
    for copy in copies:
        copy.start()


def wait(copies):
    for copy in copies:
        copy.wait()


def send_kernel(src_ref, *refs):
    far, x_ref, outs_far, near, near_out, sem = refs[:4], refs[4], refs[5:8], refs[8:12], refs[12:15], refs[15]
    sel_ref, gsel_ref, gates_ref = near_out
    copies, at = [], 0
    for src, dst, n in zip(far, near, (1, 4, 4, 2)):
        copies.append(chunked(src, dst, n, sem, at))
        at += n
    back = [pltpu.make_async_copy(a, b, sem.at[at + i]) for i, (a, b) in enumerate(zip(near_out, outs_far))]
    for i in (0, 3, 1, 2):
        start(copies[i])
    table_ref, tok_ref, grad_ref, router_ref = near
    tok_count, width = tok_ref.shape
    experts, cap = table_ref.shape
    n_dp, slots, _ = x_ref.shape
    chunks = slots // (experts * MOST)
    cols = width // n_dp
    wait(copies[0])
    table = table_ref[...]
    owner = table // tok_count
    offset = table - owner * tok_count
    mine = (owner == src_ref[0]).astype(F32)
    before = (iota((cap, cap), 0) < iota((cap, cap), 1)).astype(BF16)
    rank = nn(mine.astype(BF16), before)
    col = iota((experts, slots), 1)
    own_col = (col // (MOST * chunks)) == iota((experts, slots), 0)
    col_rank = (col // chunks) % MOST
    wanted = jnp.zeros((1, slots), F32)
    for m in range(MOST):
        chosen = jnp.sum(
            jnp.where(rank == m, mine, 0.0) * (offset + 1).astype(F32), axis=1, keepdims=True
        )
        wanted += jnp.sum(
            jnp.where(own_col & (col_rank == m), chosen, 0.0), axis=0, keepdims=True
        )
    sel = (iota((tok_count, slots), 0) + 1).astype(F32) == wanted
    wait(copies[3])
    wait(copies[1])
    gates = jax.nn.sigmoid(nt(tok_ref[...], router_ref[...]))
    gates_ref[...] = gates
    expand = own_col.astype(BF16)
    gate_exp = sum(nn(p, expand) for p in pieces(gates))
    gsel = jnp.where(sel, gate_exp, 0.0)
    sel_low = sel.astype(BF16)
    sel_ref[...] = sel_low
    gsel_ref[...] = gsel
    start(back)
    ones = jnp.ones((tok_count, LANES), BF16)
    slot_gate = sum(tn(p, ones) for p in pieces(gsel))
    slot_empty = (1.0 - tn(sel_low, ones)) * EMPTY
    chunk = iota((tok_count, slots), 1) % chunks
    pick = jnp.concatenate(
        [jnp.where(chunk == c, sel_low, jnp.zeros_like(sel_low)) for c in range(chunks)], axis=0
    )
    wait(copies[2])
    for d in range(n_dp):
        parts = []
        for c in range(chunks):
            span = slice(d * cols + c * LANES, d * cols + (c + 1) * LANES)
            parts.append(jnp.concatenate([tok_ref[:, span], grad_ref[:, span]], axis=1))
        got = tn(pick, jnp.concatenate(parts, axis=0))
        x_ref[d, :, :LANES] = (got[:, :LANES] + slot_empty).astype(BF16)
        x_ref[d, :, LANES:] = (got[:, LANES:] * slot_gate).astype(BF16)
    wait(back)


def pack_kernel(x_ref, down_ref, p_ref, gated_ref, pick_ref):
    n_dp, rows_all, cols = p_ref.shape
    rows_n = gated_ref.shape[0]
    half = rows_all - rows_n
    cap = rows_n // n_dp
    chunks = cols // LANES
    slots = x_ref.shape[0] // n_dp
    lane = iota((slots, LANES), 1)
    row = iota((slots, LANES), 0)
    held = [x_ref[g * slots : (g + 1) * slots, :LANES] < EMPTY / 2 for g in range(n_dp)]
    a, b = iota((slots, slots), 0), iota((slots, slots), 1)
    before = ((b // chunks < a // chunks) & (b % chunks == 0)).astype(BF16)
    place = nn(before, jnp.concatenate([h.astype(BF16) for h in held], axis=1))
    mine = lane // cap == row % chunks
    want = (lane % cap).astype(F32)
    for g in range(n_dp):
        at = jnp.where(mine, place[:, g * LANES : (g + 1) * LANES], -1.0)
        pick = jnp.where(at == want, held[g].astype(F32), 0.0).astype(BF16)
        pick_ref[g * slots : (g + 1) * slots, :] = pick
        y = tn(pick, x_ref[g * slots : (g + 1) * slots, :]).astype(BF16)
        own = slice(g * cap, (g + 1) * cap)
        for c in range(chunks):
            span = slice(c * LANES, (c + 1) * LANES)
            gated_ref[own, span] = y[c * cap : (c + 1) * cap, LANES:]
            for d in range(n_dp):
                p_ref[d, own, span] = y[c * cap : (c + 1) * cap, :LANES]
    gated = gated_ref[...]
    for d in range(n_dp):
        term = nt(down_ref[2 * d * half : 2 * (d + 1) * half, :], gated).astype(BF16)
        p_ref[d, rows_n:, :rows_n] = term[:half]
        p_ref[d, rows_n:, rows_n:] = term[half:]


def hidden_kernel(src_ref, a_ref, gate_ref, up_ref, router_ref, dh_ref, du_ref, act_ref, lines_ref):
    units, width = gate_ref.shape
    experts = router_ref.shape[0]
    n_dp, rows_all, cols = a_ref.shape
    half = units // 2
    rows_n = rows_all - half
    total = jnp.zeros((2 * units + experts, rows_n), F32)
    dact = jnp.zeros((units, rows_n), F32)
    group = 2
    for d in range(0, n_dp, group):
        span = slice(d * cols, (d + group) * cols)
        left = jnp.concatenate([gate_ref[:, span], up_ref[:, span], router_ref[:, span]], axis=0)
        rows = jnp.concatenate([a_ref[d + i, :rows_n, :] for i in range(group)], axis=1)
        total += nt(left, rows)
    for d in range(n_dp):
        term = a_ref[d, rows_n:, :].astype(F32)
        dact += jnp.concatenate([term[:, :rows_n], term[:, rows_n:]], axis=0)
    h, u, logits = total[:units], total[units : 2 * units], total[2 * units :]
    own = jnp.where(iota(logits.shape, 0) == src_ref[0], logits, 0.0)
    gate = jax.nn.sigmoid(jnp.sum(own, axis=0, keepdims=True))
    sig = jax.nn.sigmoid(h)
    act = (h * sig * u).astype(BF16)
    dh = (dact * u * sig * (1.0 + h * (1.0 - sig))).astype(BF16)
    du = (dact * h * sig).astype(BF16)
    dh_ref[...] = dh
    du_ref[...] = du
    dlogit = jnp.sum(act.astype(F32) * dact, axis=0, keepdims=True) * (1.0 - gate)
    lines = [p.astype(F32) for p in pieces(dlogit)]
    extra = lines_ref.shape[0]
    lines.append(jnp.zeros((extra - len(lines), rows_n), F32))
    lines = jnp.concatenate(lines, axis=0)
    lines_ref[...] = jnp.concatenate([lines, jnp.zeros((extra, cols - rows_n), F32)], axis=1).astype(BF16)
    act_ref[...] = act


def diff_kernel(dh_ref, du_ref, act_ref, lines_ref, gate_ref, up_ref, c_ref):
    units, rows_n = act_ref.shape
    n_dp, _, cols = c_ref.shape
    half = units // 2
    rows_all = rows_n + half
    act, lines = act_ref[...], lines_ref[...]
    dht, dut = dh_ref[...].T, du_ref[...].T
    for d in range(n_dp):
        span = slice(d * cols, (d + 1) * cols)
        c_ref[d, :rows_n, :] = (nn(dht, gate_ref[:, span]) + nn(dut, up_ref[:, span])).astype(BF16)
        c_ref[d, rows_n:rows_all, :rows_n] = act[:half]
        c_ref[d, rows_n:rows_all, rows_n:] = act[half:]
        c_ref[d, rows_all:, :] = lines


def back_kernel(c_ref, a_ref, down_ref, pick_ref, z_out, r_ref, act_out, z_ref, act_ref, sem):
    n_dp, rows_all, cols = a_ref.shape
    half = act_ref.shape[0] // (2 * n_dp)
    rows_n = rows_all - half
    cap = rows_n // n_dp
    chunks = cols // LANES
    slots = z_ref.shape[0] // n_dp
    diff = jnp.zeros((rows_n, cols), F32)
    packed = jnp.zeros((c_ref.shape[1] - rows_all, cols), F32)
    for d in range(n_dp):
        act_ref[2 * d * half : (2 * d + 1) * half, :] = c_ref[d, rows_n:rows_all, :rows_n]
        act_ref[(2 * d + 1) * half : 2 * (d + 1) * half, :] = c_ref[d, rows_n:rows_all, rows_n:]
        diff += c_ref[d, :rows_n, :].astype(F32)
        packed += c_ref[d, rows_all:, :].astype(F32)
    copies = [pltpu.make_async_copy(act_ref, act_out, sem.at[n_dp])]
    copies[0].start()
    diff = diff.astype(BF16)
    out = tn(act_ref[...], down_ref[...]).astype(BF16)
    for g in range(n_dp):
        own = slice(g * cap, (g + 1) * cap)
        y = jnp.concatenate(
            [
                jnp.concatenate([x[own, c * LANES : (c + 1) * LANES] for x in (out, diff)], axis=1)
                for c in range(chunks)
            ],
            axis=0,
        )
        at = slice(g * slots, (g + 1) * slots)
        z_ref[at, :] = nn(pick_ref[at, :], y).astype(BF16)
        copies.append(pltpu.make_async_copy(z_ref.at[at], z_out.at[at], sem.at[g]))
        copies[-1].start()
    dlogit = packed[:1, :rows_n] + packed[1:2, :rows_n]
    terms = [p.astype(F32) for p in pieces(dlogit)]
    terms = jnp.concatenate(terms + [jnp.zeros((8 - len(terms), rows_n), F32)], axis=0).astype(BF16)
    part = r_ref.shape[1]
    lines = []
    for d in range(n_dp):
        line = jnp.sum(nn(terms, a_ref[d, :rows_n, :]), axis=0, keepdims=True)
        lines += [line[:, i : i + part] for i in range(0, cols, part)]
    r_ref[...] = jnp.concatenate(lines, axis=0).astype(BF16)
    for copy in copies:
        copy.wait()


def weight_kernel(dh_ref, du_ref, act_ref, gated_ref, a_ref, gg_ref, ug_ref, dg_ref):
    n_dp, _, cols = a_ref.shape
    rows_n = gated_ref.shape[0]
    dh, du, gated = dh_ref[...], du_ref[...], gated_ref[...]
    for d in range(n_dp):
        span = slice(d * cols, (d + 1) * cols)
        rows = a_ref[d, :rows_n, :]
        gg_ref[:, span] = nn(dh, rows).astype(BF16)
        ug_ref[:, span] = nn(du, rows).astype(BF16)
    step = 256
    for j in range(0, dg_ref.shape[0], step):
        dg_ref[j : j + step, :] = nn(act_ref[j : j + step, :], gated).astype(BF16)


def take_kernel(src_ref, r_ref, *refs):
    far, outs_far, near, near_out, sem = refs[:6], refs[6:9], refs[9:15], refs[15:18], refs[18]
    d_ref, sel_ref, gsel_ref, gates_ref, grad_ref, router_ref = near
    mixed_ref, tgrad_ref, rgrad_ref = near_out
    copies, at = [], 0
    for a, b, n in zip(far, near, (4, 1, 1, 1, 1, 1)):
        copies.append(chunked(a, b, n, sem, at))
        at += n
    for i in (1, 2, 0, 4, 3, 5):
        start(copies[i])
    tok_count, width = grad_ref.shape
    experts = gates_ref.shape[1]
    slots = sel_ref.shape[1]
    n_dp = d_ref.shape[0] // slots
    chunks = slots // (experts * MOST)
    cols = width // n_dp
    rgrad_back = chunked(rgrad_ref, outs_far[2], 1, sem, at)
    at += 1

    def column_copies(i, at):
        blocks = [pl.ds(d * cols, 2 * cols) for d in range(0, n_dp, 2)]
        return [
            pltpu.make_async_copy(near_out[i].at[:, b], outs_far[i].at[:, b], sem.at[at + d])
            for d, b in enumerate(blocks)
        ]

    mixed_back = column_copies(0, at)
    tgrad_back = column_copies(1, at + n_dp)
    chunk = iota((tok_count, slots), 1) % chunks

    def by_chunk(x):
        return jnp.concatenate(
            [jnp.where(chunk == c, x, jnp.zeros_like(x)) for c in range(chunks)], axis=0
        )

    def span(d, c):
        return slice(d * cols + c * LANES, d * cols + (c + 1) * LANES)

    def both(d, lanes):
        return jnp.concatenate(
            [d_ref[i * slots : (i + 1) * slots, lanes] for i in (d, d + 1)], axis=1
        )

    wait(copies[1])
    wait(copies[2])
    pick = by_chunk(sel_ref[...])
    weights = [by_chunk(w) for w in pieces(gsel_ref[...])]
    hits = jnp.zeros(pick.shape, F32)
    diffs = []
    for d in range(0, n_dp, 2):
        wait(copies[0][d // 2 : d // 2 + 1])
        outs = both(d, slice(0, LANES))
        mixed = sum(nn(w, outs) for w in weights).astype(BF16)
        for i in range(2):
            for c in range(chunks):
                mixed_ref[:, span(d + i, c)] = mixed[
                    c * tok_count : (c + 1) * tok_count, i * LANES : (i + 1) * LANES
                ]
        mixed_back[d // 2].start()
        if d == 0:
            wait(copies[4])
        grads = jnp.concatenate(
            [
                jnp.concatenate([grad_ref[:, span(d + i, c)] for i in range(2)], axis=1)
                for c in range(chunks)
            ],
            axis=0,
        )
        hits += nt(grads, outs)
        diffs.append(nn(pick, both(d, slice(LANES, 2 * LANES))))
    n_rows, part = r_ref.shape
    lines = n_rows // experts
    me = src_ref[0]
    me_x, me_z = me // 8, (me // 2) % 4
    row, col = iota((n_rows, n_rows), 0), iota((n_rows, n_rows), 1)
    block = col // lines
    source = ((me_x + 4 - (block // 2) % 4) % 4) * 8 + ((me_z + 4 - block // 8) % 4) * 2 + block % 2
    sort = ((row % experts == source) & (row // experts == col % lines)).astype(BF16)
    rgrad = nn(sort, r_ref[...])
    for i in range(lines):
        rgrad_ref[:, i * part : (i + 1) * part] = rgrad[i * experts : (i + 1) * experts]
    start(rgrad_back)
    hits = jnp.where(pick != 0, hits, 0.0)
    hits = sum(hits[c * tok_count : (c + 1) * tok_count] for c in range(chunks))
    collect = (iota((slots, experts), 0) // (MOST * chunks) == iota((slots, experts), 1)).astype(BF16)
    wait(copies[3])
    wait(copies[5])
    gates = gates_ref[...]
    dlogit = sum(nn(p, collect) for p in pieces(hits)) * gates * (1.0 - gates)
    terms = jnp.concatenate(pieces(dlogit), axis=1)
    for d in range(0, n_dp, 2):
        router = router_ref[:, d * cols : (d + 2) * cols]
        from_router = nn(terms, jnp.concatenate([router] * 2, axis=0))
        for i in range(2):
            for c in range(chunks):
                at = i * cols + c * LANES
                tgrad_ref[:, span(d + i, c)] = (
                    diffs[d // 2][c * tok_count : (c + 1) * tok_count, i * LANES : (i + 1) * LANES]
                    + from_router[:, at : at + LANES]
                ).astype(BF16)
        tgrad_back[d // 2].start()
    wait(rgrad_back)
    wait(mixed_back)
    wait(tgrad_back)


def shifted(x, k, to):
    return lax.ppermute(x, "expert", [(e, to(e, k)) for e in range(32)])


def paired(x, axis):
    got = shifted(x, 1, lambda e, k: e ^ k)
    first = lax.axis_index("expert") % 2 == 0
    return jnp.where(first, jnp.concatenate([x, got], axis), jnp.concatenate([got, x], axis))


def spread(r):
    def along_x(e, k):
        return (e + 8 * k) % 32

    def along_z(e, k):
        return e // 8 * 8 + (e + 2 * k) % 8

    r = paired(r, 0)
    r = jnp.concatenate([r] + [shifted(r, k, along_x) for k in range(1, 4)], axis=0)
    middle = r.shape[1] // 2
    half = jnp.where(lax.axis_index("expert") % 2 == 0, r[:, :middle], r[:, middle:])
    return jnp.concatenate([half] + [shifted(half, k, along_z) for k in range(1, 4)], axis=0)


def local(tokens, out_grad, router, choice_index, gate_weight, up_weight, down_weight):
    tok, grad, table = tokens[0], out_grad[0], choice_index[0]
    gate, up, down = gate_weight[0], up_weight[0], down_weight[0]
    router = router.T
    tok_count, width = tok.shape
    experts, cap = table.shape
    units, cols = gate.shape[0], down.shape[1]
    n_dp = lax.axis_size("dp")
    rows_n = n_dp * cap
    chunks = cols // LANES
    per = MOST * chunks
    slots = experts * per
    rows_all = rows_n + units // 2
    src = lax.axis_index("expert").astype(jnp.int32).reshape(1)

    def swap(x, axis):
        return lax.all_to_all(x, axis, split_axis=0, concat_axis=0, tiled=True)

    kept = [((tok_count, slots), BF16), ((tok_count, slots), F32), ((tok_count, experts), F32)]
    x, sel, gsel, gates = call(
        send_kernel,
        [((n_dp, slots, 2 * LANES), BF16)] + kept,
        (src, table, tok, grad, router),
        far_in=(1, 2, 3, 4),
        far_out=(1, 2, 3),
        scratch=[pltpu.VMEM(a.shape, a.dtype) for a in (table, tok, grad, router)]
        + [pltpu.VMEM(s, d) for s, d in kept]
        + [pltpu.SemaphoreType.DMA((11 + len(kept),))],
    )
    x = swap(x.reshape(n_dp * experts, per, 2 * LANES), ("dp", "expert"))
    a, gated, pick = call(
        pack_kernel,
        [
            ((n_dp, rows_all, cols), BF16),
            ((rows_n, cols), BF16),
            ((n_dp * slots, LANES), BF16),
        ],
        (x.reshape(n_dp * slots, 2 * LANES), down),
    )
    a = swap(a, "dp")
    dh, du, act, lines = call(
        hidden_kernel,
        [((units, rows_n), BF16)] * 3 + [((16, cols), BF16)],
        (src, a, gate, up, router),
    )
    (c,) = call(
        diff_kernel, [((n_dp, rows_all + 16, cols), BF16)], (dh, du, act, lines, gate, up)
    )
    c = swap(c, "dp")
    z, r, act = call(
        back_kernel,
        [
            ((n_dp * slots, 2 * LANES), BF16),
            ((16, width // 16), BF16),
            ((n_dp * units, rows_n), BF16),
        ],
        (c, a, down, pick),
        far_out=(0, 2),
        scratch=[
            pltpu.VMEM((n_dp * slots, 2 * LANES), BF16),
            pltpu.VMEM((n_dp * units, rows_n), BF16),
            pltpu.SemaphoreType.DMA((n_dp + 1,)),
        ],
    )
    z = swap(z.reshape(n_dp * experts, per, 2 * LANES), ("dp", "expert"))
    r = spread(r)
    gate_grad, up_grad, down_grad = call(
        weight_kernel,
        [((units, width), BF16), ((units, width), BF16), ((n_dp * units, cols), BF16)],
        (dh, du, act, gated, a),
    )
    taken = (z.reshape(n_dp * slots, 2 * LANES), sel, gsel, gates, grad, router)
    r, gate_grad, up_grad, down_grad = lax.optimization_barrier((r, gate_grad, up_grad, down_grad))
    r = paired(r, 1)
    results = [((tok_count, width), BF16), ((tok_count, width), BF16), ((experts, width), F32)]
    mixed, token_grad, router_grad = call(
        take_kernel,
        results,
        (src, r) + taken,
        far_in=range(2, 8),
        far_out=range(3),
        scratch=[pltpu.VMEM(a.shape, a.dtype) for a in taken]
        + [pltpu.VMEM(s, d) for s, d in results]
        + [pltpu.SemaphoreType.DMA((21 + 2 * n_dp,))],
    )
    return (
        mixed[None],
        token_grad[None],
        router_grad.T,
        gate_grad[None],
        up_grad[None],
        down_grad[None],
    )


def solution(mesh):
    in_specs = (
        P("dp", "expert", None),
        P("dp", "expert", None),
        P(),
        P("dp", None, None),
        P("expert", "dp", None),
        P("expert", "dp", None),
        P("expert", None, "dp"),
    )
    out_specs = (
        P("dp", "expert", None),
        P("dp", "expert", None),
        P(),
        P("expert", "dp", None),
        P("expert", "dp", None),
        P("expert", None, "dp"),
    )
    return jax.shard_map(local, mesh=mesh, in_specs=in_specs, out_specs=out_specs, check_vma=False)
```
